128 devices in a mesh: row: 4 (over z), col: 8 (over y, core), slide: 4 (over x).
Axes of the slice: x: 4, y: 4, z: 4, core: 2. Of those that a mesh axis runs over, the one named last changes fastest.
Arguments:
- image: bfloat16 [4, 384, 768, 256], P('slide', 'row', 'col'), may hold values from -48 to 48
- reduce_weight: bfloat16 [256, 128], replicated, may hold values from -0.375 to 0.375
- spatial_weight: bfloat16 [3, 3, 128, 128], replicated, may hold values from -0.1875 to 0.1875
- expand_weight: bfloat16 [128, 512], replicated, may hold values from -0.5 to 0.5
- project_weight: bfloat16 [256, 512], replicated, may hold values from -0.375 to 0.375
- classify_weight: float32 [512, 2], replicated, may hold values from -0.6 to 0.6
- tissue_mask: int32 [4, 12, 24], P('slide'), may hold values from 0 to 1, as said below
- slide_labels: int32 [4], P('slide'), may hold values from 0 to 1
Outputs:
- grad_image: bfloat16 [4, 384, 768, 256], P('slide', 'row', 'col')
- grad_reduce: float32 [256, 128], replicated
- grad_spatial: float32 [3, 3, 128, 128], replicated
- grad_expand: float32 [128, 512], replicated
- grad_project: float32 [256, 512], replicated
- grad_classify: float32 [512, 2], replicated
- loss: float32 [], replicated
The draws below stay inside these ranges and needn't reach their ends.
Inputs may be any that keep to these rules, and one draw needn't show every extreme that they name: `tissue_mask`: 1 marks a tissue tile and 0 background; every slide has at least one tissue tile.
All inputs are finite; a program needn't handle non-finite values.
Results may differ from the reference program's by a relative error of at most 0.0095.
Values may be sent and summed in bfloat16 or wider, within the bound.
A program may use at most 128 MiB of HBM per device.

```python
import math
import jax
import jax.numpy as jnp
from jax import lax

CI = 256
CM = 128
CO = 512
NCLS = 2
BLK = 32
BR = 3
BC = 3
SLIDES = 4
MR = 12
MC = 24
NH = 384
NW = 768
TB = 16


def draw_image(key, part):
    key = jax.random.fold_in(key, 11)
    base_key, pixel_key, channel_key = jax.random.split(key, 3)
    full_shape = (SLIDES, NH, NW, CI)
    pixel_scale = jnp.exp(jax.random.uniform(pixel_key, (SLIDES, NH, NW, 1), jnp.float32, math.log(0.3), math.log(3.0)))
    channel_scale = jnp.exp(jax.random.uniform(channel_key, (CI,), jnp.float32, math.log(0.4), math.log(4.0)))
    row_groups = MR // BR
    col_groups = MC // BC
    device_count = SLIDES * row_groups * col_groups
    slide_pos = lax.broadcasted_iota(jnp.int32, full_shape, 0)
    row_pos = lax.broadcasted_iota(jnp.int32, full_shape, 1) // (BR * BLK)
    col_pos = lax.broadcasted_iota(jnp.int32, full_shape, 2) // (BC * BLK)
    channel_pos = lax.broadcasted_iota(jnp.int32, full_shape, 3)
    holder = (slide_pos * row_groups + row_pos) * col_groups + col_pos
    owner_scale = jnp.where(channel_pos % device_count == holder, 1.0, 0.1).astype(jnp.float32)
    values = jnp.clip(jax.random.normal(base_key, full_shape, jnp.float32), -4.0, 4.0) * pixel_scale * channel_scale
    return (values * owner_scale).astype(jnp.bfloat16)


def draw_tissue_mask(key, part):
    key = jax.random.fold_in(key, 23)
    roll_key, forced_key = jax.random.split(key, 2)
    dice_rolls = jax.random.randint(roll_key, (SLIDES, MR, MC), 0, 100)
    columns = lax.broadcasted_iota(jnp.int32, (SLIDES, MR, MC), 2)
    row_index = lax.broadcasted_iota(jnp.int32, (SLIDES, MR, MC), 1)
    threshold = 15 + 80 * columns // max(MC - 1, 1)
    tissue = (dice_rolls < threshold).astype(jnp.int32)
    forced_tile = jax.random.randint(forced_key, (SLIDES, 1, 1), 0, MR * MC)
    tissue = jnp.where(row_index * MC + columns == forced_tile, 1, tissue)
    return tissue.astype(jnp.int32)


def with_ends(drawn, stream_key, least, top_value):
    index_at = [jax.random.randint(jax.random.fold_in(stream_key, axis), (), 0, length) for axis, length in enumerate(drawn.shape)]
    widest = drawn.shape.index(max(drawn.shape))
    next_to = index_at[:widest] + [(index_at[widest] + 1) % drawn.shape[widest]] + index_at[widest + 1:]
    return drawn.at[tuple(index_at)].set(least).at[tuple(next_to)].set(top_value)


def noise(rng, extent, width, limit, held_as=jnp.bfloat16):
    return jnp.clip(width * jax.random.normal(rng, extent, jnp.float32), -limit, limit).astype(held_as)


def setup_inputs(seed: int = 0) -> dict:
    streams_of = jax.random.split(jax.random.key(seed), 9)
    return {
        "image": draw_image(jax.random.fold_in(streams_of[8], 71), 0),
        "reduce_weight": noise(streams_of[1], (CI, CM), CI ** -0.5, 0.375),
        "spatial_weight": noise(streams_of[2], (3, 3, CM, CM), (9 * CM) ** -0.5, 0.1875),
        "expand_weight": noise(streams_of[3], (CM, CO), CM ** -0.5, 0.5),
        "project_weight": noise(streams_of[4], (CI, CO), CI ** -0.5, 0.375),
        "classify_weight": noise(streams_of[5], (CO, NCLS), 0.1, 0.6, jnp.float32),
        "tissue_mask": draw_tissue_mask(jax.random.fold_in(streams_of[8], 71), 0),
        "slide_labels": with_ends(jax.random.randint(streams_of[7], (SLIDES,), 0, 2), jax.random.fold_in(streams_of[7], 1), 0, 1).astype(jnp.int32),
    }


EPSILON = 1e-05

def normed(values):
    return values * lax.rsqrt(lax.optimization_barrier(jnp.mean(values * values, axis=-1, keepdims=True)) + EPSILON)

def activate(values):
    return jax.nn.silu(normed(values))

def gather_taps(padded, out_rows, out_cols):
    channels = padded.shape[-1]
    grid_view = padded.reshape(out_rows + 1, 2, out_cols + 1, 2, channels)
    pieces = []
    for row_tap in range(3):
        for col_tap in range(3):
            pieces.append(grid_view[row_tap // 2:row_tap // 2 + out_rows, row_tap % 2, col_tap // 2:col_tap // 2 + out_cols, col_tap % 2])
    return jnp.concatenate(pieces, axis=-1)

def spread_taps(grads, spatial_flat):
    grad_rows, grad_cols, channels = grads.shape
    tap_terms = jnp.dot(grads.reshape(-1, channels), spatial_flat.T, preferred_element_type=jnp.float32)
    tap_terms = tap_terms.reshape(grad_rows, grad_cols, 3, 3, channels)
    parity_sums = [[None, None], [None, None]]
    for row_tap in range(3):
        for col_tap in range(3):
            placed = jnp.pad(tap_terms[:, :, row_tap, col_tap], ((row_tap // 2, 1 - row_tap // 2), (col_tap // 2, 1 - col_tap // 2), (0, 0)))
            if parity_sums[row_tap % 2][col_tap % 2] is None:
                parity_sums[row_tap % 2][col_tap % 2] = placed
            else:
                parity_sums[row_tap % 2][col_tap % 2] = parity_sums[row_tap % 2][col_tap % 2] + placed
    upper_half = jnp.stack([parity_sums[0][0], parity_sums[0][1]], axis=2)
    lower_half = jnp.stack([parity_sums[1][0], parity_sums[1][1]], axis=2)
    assembled = jnp.stack([upper_half, lower_half], axis=1)
    return assembled.reshape(2 * grad_rows + 2, 2 * grad_cols + 2, channels)

def reference(image, reduce_weight, spatial_weight, expand_weight, project_weight, classify_weight, tissue_mask, slide_labels):
    spatial_flat = spatial_weight.reshape(9 * CM, CM)
    tile_scale = float(MR * MC)
    half_rows = NH // 2
    half_cols = NW // 2
    highest = lax.Precision.HIGHEST

    def one_slide(inputs):
        pixels, mask_tiles, label = inputs
        pre_reduce = jnp.dot(pixels.reshape(-1, CI), reduce_weight, preferred_element_type=jnp.float32).reshape(NH, NW, CM)
        reduced = activate(pre_reduce).astype(jnp.bfloat16)
        padded = jnp.pad(reduced, ((1, 1), (1, 1), (0, 0)))
        patches = gather_taps(padded, half_rows, half_cols)
        pre_spatial = jnp.dot(patches.reshape(-1, 9 * CM), spatial_flat, preferred_element_type=jnp.float32).reshape(half_rows, half_cols, CM)
        spatial = activate(pre_spatial).astype(jnp.bfloat16)
        even_pixels = pixels.reshape(half_rows, 2, half_cols, 2, CI)[:, 0, :, 0]
        pre_expand = jnp.dot(spatial.reshape(-1, CM), expand_weight, preferred_element_type=jnp.float32).reshape(half_rows, half_cols, CO)
        pre_project = jnp.dot(even_pixels.reshape(-1, CI), project_weight, preferred_element_type=jnp.float32).reshape(half_rows, half_cols, CO)
        combined = normed(pre_expand) + normed(pre_project)
        merged = jax.nn.silu(combined)
        features = merged.reshape(MR, TB, MC, TB, CO).mean(axis=(1, 3))
        logits = jnp.dot(features.reshape(-1, CO), classify_weight, precision=highest).reshape(MR, MC, NCLS)
        label_sign = 1.0 - 2.0 * label.astype(jnp.float32)
        margin = (logits[..., 1] - logits[..., 0]) * label_sign
        tissue = mask_tiles.astype(jnp.float32)
        tissue_tiles = jnp.sum(tissue)
        loss_part = jnp.sum(tissue * jnp.logaddexp(0.0, margin)) / tissue_tiles
        tile_weight = tissue * jax.nn.sigmoid(margin) / tissue_tiles
        logit_grad = jnp.stack([-tile_weight * label_sign, tile_weight * label_sign], axis=-1)
        part_classify = jnp.dot(features.reshape(-1, CO).T, logit_grad.reshape(-1, NCLS), precision=highest)
        feature_grad = jnp.dot(logit_grad.reshape(-1, NCLS), classify_weight.T, precision=highest).reshape(MR, MC, CO) * tile_scale
        spread_grad = jnp.broadcast_to(feature_grad[:, None, :, None, :], (MR, TB, MC, TB, CO)).reshape(half_rows, half_cols, CO)
        merged_grad = jax.vjp(jax.nn.silu, combined)[1](spread_grad)[0]
        expand_grad = jax.vjp(normed, pre_expand)[1](merged_grad)[0].astype(jnp.bfloat16)
        project_grad = jax.vjp(normed, pre_project)[1](merged_grad)[0].astype(jnp.bfloat16)
        part_expand = jnp.dot(spatial.reshape(-1, CM).T, expand_grad.reshape(-1, CO), preferred_element_type=jnp.float32)
        part_project = jnp.dot(even_pixels.reshape(-1, CI).T, project_grad.reshape(-1, CO), preferred_element_type=jnp.float32)
        spatial_grad = jnp.dot(expand_grad.reshape(-1, CO), expand_weight.T, preferred_element_type=jnp.float32).reshape(half_rows, half_cols, CM)
        pre_spatial_grad = jax.vjp(activate, pre_spatial)[1](spatial_grad)[0].astype(jnp.bfloat16)
        part_spatial = jnp.dot(patches.reshape(-1, 9 * CM).T, pre_spatial_grad.reshape(-1, CM), preferred_element_type=jnp.float32)
        spread = spread_taps(pre_spatial_grad, spatial_flat)
        reduced_grad = spread[1:NH + 1, 1:NW + 1]
        pre_reduce_grad = jax.vjp(activate, pre_reduce)[1](reduced_grad)[0].astype(jnp.bfloat16)
        part_reduce = jnp.dot(pixels.reshape(-1, CI).T, pre_reduce_grad.reshape(-1, CM), preferred_element_type=jnp.float32)
        main_grad = jnp.dot(pre_reduce_grad.reshape(-1, CM), reduce_weight.T, preferred_element_type=jnp.float32).reshape(NH, NW, CI)
        side_grad = jnp.dot(project_grad.reshape(-1, CO), project_weight.T, preferred_element_type=jnp.float32).reshape(half_rows, half_cols, CI)
        side_full = jnp.pad(side_grad[:, None, :, None, :], ((0, 0), (0, 1), (0, 0), (0, 1), (0, 0))).reshape(NH, NW, CI)
        slide_grad = (main_grad + side_full).astype(jnp.bfloat16)
        return (slide_grad, part_reduce, part_spatial, part_expand, part_project, part_classify, loss_part)
    results = lax.map(one_slide, (image, tissue_mask, slide_labels))
    grad_image, parts_reduce, parts_spatial, parts_expand, parts_project, parts_classify, losses = results
    return (grad_image, lax.optimization_barrier(jnp.sum(parts_reduce, axis=0)) / tile_scale, lax.optimization_barrier(jnp.sum(parts_spatial, axis=0)).reshape(3, 3, CM, CM) / tile_scale, lax.optimization_barrier(jnp.sum(parts_expand, axis=0)) / tile_scale, lax.optimization_barrier(jnp.sum(parts_project, axis=0)) / tile_scale, lax.optimization_barrier(jnp.sum(parts_classify, axis=0)), jnp.sum(losses))
```

```python
import jax
import jax.numpy as jnp
from jax import lax
from jax.experimental import pallas as pl
from jax.experimental.pallas import tpu as pltpu
from jax.sharding import PartitionSpec as P

EPSILON = 1e-05
MESH = pl.DeviceIdType.MESH
F32 = jnp.float32
BF16 = jnp.bfloat16

NR, NC, NS = 4, 8, 4
H = 96
Q = 48
CI, CM, CO = 256, 128, 512
TB = 16
SCALE = 1.0 / 288.0
CHUNK = 384
PIECE = CHUNK // (NR * NS)
IMG_CHUNKS = 12


def dot(a, b):
    return lax.dot_general(a, b, (((1,), (0,)), ((), ())), preferred_element_type=F32)


def dot_nt(a, b):
    return lax.dot_general(a, b, (((1,), (1,)), ((), ())), preferred_element_type=F32)


def dot_tn(a, b):
    return lax.dot_general(a, b, (((0,), (0,)), ((), ())), preferred_element_type=F32)


def lane_mean(x, n):
    return jnp.sum(x, axis=-1, keepdims=True) * (1.0 / n)


def rms_scale(v, n):
    return lax.rsqrt(lane_mean(v * v, n) + EPSILON)


def act(v):
    half = v * (0.5 * rms_scale(v, CM))
    return half * jnp.tanh(half) + half


def silu_slope(half):
    t = jnp.tanh(half)
    return (0.5 + 0.5 * t) * (1.0 + half * (1.0 - t))


def act_vjp(v, g):
    r = rms_scale(v, CM)
    n = v * r
    dn = g * silu_slope(0.5 * n)
    return r * (dn - n * lane_mean(dn * n, CM))


def loop(n, body):
    def step(i, carry):
        body(i)
        return carry

    lax.fori_loop(0, n, step, 0)


def kernel(
    img_hbm, wr, ws, we, wp, wc, mask, label,
    gimg_hbm, o_reduce, o_spatial, o_expand, o_project, o_classify, o_loss,
    img, pre, actb, rc_odd, rc_even, evp, evb, colb, col16, hcol, hcor, hcolf, srow,
    psp, spat, ne, npj, rs, feat, gb, eg, pg, dbuf, dcat, wback, eo, natb, prg16,
    dright, dcor, drightf, drow, dcol, ob,
    a_ws, a_we, a_wp, a_wr, a_misc,
    s1, r1, a1, r2, a3, s3, r4, s5, r5, a5, r6, r7,
    sem_in, sem_out, sem_h, sem_g, sem1, sem2, sem3, sem4, sem5, sem6, sem7,
):
    row, col, sld = lax.axis_index("row"), lax.axis_index("col"), lax.axis_index("slide")
    grp = row * NS + sld
    has_up, has_down = row > 0, row < NR - 1
    has_left, has_right = col > 0, col < NC - 1

    rows_in = H // IMG_CHUNKS

    def image_copy(k):
        return pltpu.make_async_copy(
            img_hbm.at[0, pl.ds(k * rows_in, rows_in)], img.at[pl.ds(k * rows_in, rows_in)], sem_in.at[k]
        )

    loop(IMG_CHUNKS, lambda k: image_copy(k).start())

    def col_peer(d):
        return {"col": lax.rem(col + d, NC)}

    def grp_peer(d):
        q = lax.rem(grp + d, NR * NS)
        return {"row": q // NS, "slide": lax.rem(q, NS)}

    barrier = pltpu.get_barrier_semaphore()
    loop(NC - 1, lambda d: pl.semaphore_signal(barrier, inc=1, device_id=col_peer(d + 1), device_id_type=MESH))
    loop(NR * NS - 1, lambda d: pl.semaphore_signal(barrier, inc=1, device_id=grp_peer(d + 1), device_id_type=MESH))
    to_diag = has_down & has_right
    from_diag = has_up & has_left

    @pl.when(to_diag)
    def _():
        pl.semaphore_signal(barrier, inc=1, device_id={"row": row + 1, "col": col + 1}, device_id_type=MESH)

    @pl.when(from_diag)
    def _():
        pl.semaphore_signal(barrier, inc=1, device_id={"row": row - 1, "col": col - 1}, device_id_type=MESH)

    wback[...] = jnp.zeros_like(wback)

    def tap(a, b):
        return ws[a, b * CM : (b + 1) * CM, :]

    for slot, a in ((0, 1), (1, 2), (2, 0)):
        wback[slot, 0:CM, 0:CM] = tap(a, 1)
        wback[slot, CM : 2 * CM, 0:CM] = tap(a, 2)
        wback[slot, CM : 2 * CM, CM : 2 * CM] = tap(a, 0)
    actb[:, 0:8, :] = jnp.zeros_like(actb[:, 0:8, :])
    dbuf[:, Q : Q + 8, :] = jnp.zeros_like(dbuf[:, Q : Q + 8, :])
    a_ws[...] = jnp.zeros_like(a_ws)
    a_we[...] = jnp.zeros_like(a_we)
    a_wp[...] = jnp.zeros_like(a_wp)
    a_wr[...] = jnp.zeros_like(a_wr)
    a_misc[...] = jnp.zeros_like(a_misc)

    @pl.when(jnp.logical_not(has_up))
    def _():
        rc_odd[0] = jnp.zeros_like(rc_odd[0])

    @pl.when(jnp.logical_not(has_left))
    def _():
        hcol[...] = jnp.zeros_like(hcol)

    @pl.when(jnp.logical_not(from_diag))
    def _():
        hcor[...] = jnp.zeros_like(hcor)

    @pl.when(jnp.logical_not(has_down))
    def _():
        dcat[Q] = jnp.zeros_like(dcat[Q])

    @pl.when(jnp.logical_not(has_right))
    def _():
        dright[...] = jnp.zeros_like(dright)

    @pl.when(jnp.logical_not(to_diag))
    def _():
        dcor[...] = jnp.zeros_like(dcor)

    eye = (
        lax.broadcasted_iota(jnp.int32, (CM, CM), 0) == lax.broadcasted_iota(jnp.int32, (CM, CM), 1)
    )
    wdiff = wc[:, 1:2] - wc[:, 0:1]
    drow_w = jnp.concatenate(
        [
            jnp.sum(jnp.where(eye, wdiff[k * CM : (k + 1) * CM], 0.0), axis=0, keepdims=True)
            for k in range(CO // CM)
        ],
        axis=1,
    )
    sign = 1.0 - 2.0 * label[0].astype(F32)
    tissue_all = mask[...].astype(F32)
    tiles = jnp.sum(jnp.sum(tissue_all, axis=1, keepdims=True), axis=0, keepdims=True)
    mask_r = lax.broadcasted_iota(jnp.int32, mask.shape, 0)
    mask_c = lax.broadcasted_iota(jnp.int32, mask.shape, 1)

    def pass1(k):
        image_copy(k).wait()
        x = img[pl.ds(k * 8, 8)].reshape(8 * H, CI)
        v = dot(x, wr[...])
        pre[pl.ds(k * 8, 8)] = v.reshape(8, H, CM)
        actb[:, 8 : 8 + H, :] = act(v).reshape(8, H, CM)
        for r in range(8):
            rows, at = (rc_even, k * 4 + r // 2) if r % 2 == 0 else (rc_odd, k * 4 + r // 2 + 1)
            for b in range(3):
                rows[at, :, b * CM : (b + 1) * CM] = actb[r, pl.ds(7 + b, Q, stride=2), :].astype(BF16)
            colb[pl.ds(k * 8 + r, 1), :] = actb[r, 7 + H : 8 + H, :]

    loop(IMG_CHUNKS, pass1)

    col16[...] = colb[...].astype(BF16)
    srow[...] = rc_odd[Q]

    def remote(src, dst, send, recv, device):
        return pltpu.make_async_remote_copy(
            src_ref=src, dst_ref=dst, send_sem=send, recv_sem=recv, device_id=device, device_id_type=MESH
        )

    down = remote(srow, rc_odd.at[0], sem_h.at[0], sem_h.at[1], {"row": lax.rem(row + 1, NR)})
    right = remote(col16, hcol, sem_h.at[2], sem_h.at[3], {"col": lax.rem(col + 1, NC)})
    diag = remote(
        col16.at[pl.ds(H - 16, 16)], hcor, sem_h.at[4], sem_h.at[5],
        {"row": lax.rem(row + 1, NR), "col": lax.rem(col + 1, NC)},
    )
    n_diag = jnp.where(to_diag, 1, 0) + jnp.where(from_diag, 1, 0)
    pl.semaphore_wait(barrier, NC - 1 + NR * NS - 1 + n_diag)
    forward = ((down, has_down, has_up), (right, has_right, has_left), (diag, to_diag, from_diag))
    for copy, sends, _ in forward:
        pl.when(sends)(copy.start)

    def even_rows(m):
        x = img[2 * m].astype(F32)
        for half in range(2):
            evb[half] = x[:, half * CM : (half + 1) * CM]
        for half in range(2):
            evp[m, :, half * CM : (half + 1) * CM] = evb[half, pl.ds(0, Q, stride=2), :].astype(BF16)

    loop(Q, even_rows)

    for copy, sends, takes in forward:
        pl.when(takes)(copy.wait_recv)
        pl.when(sends)(copy.wait_send)

    hcolf[0:H] = hcol[...].astype(F32)
    hcolf[H : H + 16] = hcor[...].astype(F32)
    first = lax.broadcasted_iota(jnp.int32, (16, CM), 0) == 0

    def patch_left(rows, at, value):
        old = rows[at, 0:16, 0:CM].astype(F32)
        rows[at, 0:16, 0:CM] = jnp.where(first, value, old).astype(BF16)

    patch_left(rc_odd, 0, hcolf[H + 15 : H + 16, :])

    def patch_rows(m):
        patch_left(rc_even, m, hcolf[pl.ds(2 * m, 1), :])
        patch_left(rc_odd, m + 1, hcolf[pl.ds(2 * m + 1, 1), :])

    loop(Q, patch_rows)

    npx = TB * Q

    def tile_row(u):
        i0 = u * TB

        def taps(a, at, n):
            if a == 1:
                return rc_even[pl.ds(at, n)].reshape(n * Q, 3 * CM)
            return rc_odd[pl.ds(at + a // 2, n)].reshape(n * Q, 3 * CM)

        def convolve(b):
            at = i0 + b * 8
            v = sum(dot(taps(a, at, 8), ws[a]) for a in range(3))
            psp[pl.ds(b * 8 * Q, 8 * Q), :] = v
            spat[pl.ds(b * 8 * Q, 8 * Q), :] = act(v).astype(BF16)

        loop(2, convolve)
        ne[...] = dot(spat[...], we[...])
        npj[...] = dot(evp[pl.ds(i0, TB)].reshape(npx, CI), wp[...])
        feat[...] = jnp.zeros_like(feat)

        def merge(i):
            for v in range(3):
                at = pl.ds(i * Q + v * TB, TB)
                e, p = ne[at, :], npj[at, :]
                r_e, r_p = rms_scale(e, CO), rms_scale(p, CO)
                n_e, n_p = e * r_e, p * r_p
                ne[at, :], npj[at, :] = n_e, n_p
                rs[0, at, :], rs[1, at, :] = (jnp.broadcast_to(r, (TB, CM)) for r in (r_e, r_p))
                half = 0.5 * (n_e + n_p)
                merged = half * jnp.tanh(half) + half
                feat[v] += merged[0:8] + merged[8:16]

        loop(TB, merge)

        for v in range(3):
            f = jnp.sum(feat[v], axis=0, keepdims=True) * (1.0 / (TB * TB))
            margin = jnp.sum(f * drow_w, axis=1, keepdims=True) * sign
            here = (mask_r == row * 3 + u) & (mask_c == col * 3 + v)
            tissue = jnp.where(here, tissue_all, 0.0)
            tissue = jnp.sum(jnp.sum(tissue, axis=1, keepdims=True), axis=0, keepdims=True)
            soft = jnp.maximum(margin, 0.0) + jnp.log(1.0 + jnp.exp(-jnp.abs(margin)))
            weight = tissue * (0.5 + 0.5 * jnp.tanh(0.5 * margin)) / tiles * sign
            for k in range(CO // CM):
                a_misc[k : k + 1, :] += f[:, k * CM : (k + 1) * CM] * weight
            a_misc[4:5, :] += jnp.broadcast_to(tissue * soft / tiles, (1, CM))
            gb[v : v + 1, :] = drow_w * (weight * 288.0)

        def unmerge(i):
            for v in range(3):
                at = pl.ds(i * Q + v * TB, TB)
                n_e, n_p = ne[at, :], npj[at, :]
                dn = gb[v : v + 1, :] * silu_slope(0.5 * (n_e + n_p))
                out = pl.ds(i0 * Q + i * Q + v * TB, TB)
                eg[at, :] = (rs[0, at, 0:1] * (dn - n_e * lane_mean(dn * n_e, CO))).astype(BF16)
                pg[out, :] = (rs[1, at, 0:1] * (dn - n_p * lane_mean(dn * n_p, CO))).astype(BF16)

        loop(TB, unmerge)

        a_we[...] += dot_tn(spat[...], eg[...])
        a_wp[...] += dot_tn(evp[pl.ds(i0, TB)].reshape(npx, CI), pg[pl.ds(i0 * Q, npx), :])

        def unconvolve(b):
            at = pl.ds(b * 8 * Q, 8 * Q)
            g = dot_nt(eg[at, :], we[...])
            d = act_vjp(psp[at, :], g)
            dbuf[:, 0:Q, :] = d.reshape(8, Q, CM)
            d16 = d.astype(BF16)
            dcat[pl.ds(i0 + b * 8, 8), :, 0:CM] = d16.reshape(8, Q, CM)
            for r in range(8):
                dcat[i0 + b * 8 + r, :, CM : 2 * CM] = dbuf[r, 1 : Q + 1, :].astype(BF16)
                dcol[pl.ds(i0 + b * 8 + r, 1), :] = dbuf[r, 0:1, :]
            for a in range(3):
                a_ws[:, a * 3 * CM : (a + 1) * 3 * CM] += dot_tn(d16, taps(a, i0 + b * 8, 8))

        loop(2, unconvolve)

    loop(3, tile_row)

    drow[...] = dcat[0]
    col16[0:Q] = dcol[...].astype(BF16)
    up = remote(drow, dcat.at[Q], sem_g.at[0], sem_g.at[1], {"row": lax.rem(row + NR - 1, NR)})
    left = remote(col16.at[pl.ds(0, Q)], dright, sem_g.at[2], sem_g.at[3], {"col": lax.rem(col + NC - 1, NC)})
    gaid = remote(
        col16.at[pl.ds(0, 16)], dcor, sem_g.at[4], sem_g.at[5],
        {"row": lax.rem(row + NR - 1, NR), "col": lax.rem(col + NC - 1, NC)},
    )
    backward = ((up, has_up, has_down), (left, has_left, has_right), (gaid, from_diag, to_diag))
    for copy, sends, _ in backward:
        pl.when(sends)(copy.start)

    for t in range(9):
        s1[t * CM : (t + 1) * CM, :] = a_ws[:, t * CM : (t + 1) * CM].T.astype(BF16)
    for q in range(4):
        s1[1152 + q * 128 : 1152 + (q + 1) * 128, :] = a_we[:, q * CM : (q + 1) * CM].astype(BF16)
        s1[1664 + q * 256 : 1664 + (q + 1) * 256, :] = a_wp[:, q * CM : (q + 1) * CM].astype(BF16)
    s1[2688:3072, :] = jnp.zeros((384, CM), BF16)

    for copy, sends, takes in backward:
        pl.when(takes)(copy.wait_recv)
        pl.when(sends)(copy.wait_send)

    drightf[0:Q] = dright[...].astype(F32)
    drightf[Q : Q + 16] = dcor[...].astype(F32)
    last = lax.broadcasted_iota(jnp.int32, (16, CM), 0) == 15

    def patch_right(at, value):
        old = dcat[at, Q - 16 : Q, CM : 2 * CM].astype(F32)
        dcat[at, Q - 16 : Q, CM : 2 * CM] = jnp.where(last, value, old).astype(BF16)

    loop(Q, lambda m: patch_right(m, drightf[pl.ds(m, 1), :]))
    patch_right(Q, drightf[Q : Q + 1, :])

    def pass3(b):
        i0 = b * 8
        here = dcat[pl.ds(i0, 8)].reshape(8 * Q, 2 * CM)
        below = dcat[pl.ds(i0 + 1, 8)].reshape(8 * Q, 2 * CM)
        eo[0] = dot_nt(here, wback[0]).reshape(8, Q, 2 * CM)
        eo[1] = (dot_nt(here, wback[1]) + dot_nt(below, wback[2])).reshape(8, Q, 2 * CM)

        def one_row(i):
            for rp in range(2):
                at = 2 * (i0 + i) + rp
                for cp in range(2):
                    v = pre[at, pl.ds(cp, Q, stride=2), :]
                    natb[rp, pl.ds(cp, Q, stride=2), :] = act_vjp(v, eo[rp, i, :, cp * CM : (cp + 1) * CM])
                prg16[at] = natb[rp].astype(BF16)

        loop(8, one_row)
        rows = pl.ds(2 * i0, 16)
        a_wr[...] += dot_tn(prg16[rows].reshape(16 * H, CM), img[rows].reshape(16 * H, CI))

    loop(6, pass3)

    def image_out(k):
        rows = pl.ds(k * 8, 8)
        return pltpu.make_async_copy(img.at[rows], gimg_hbm.at[0, rows], sem_out.at[k])

    def pass4(k):
        main = dot_nt(prg16[pl.ds(k * 8, 8)].reshape(8 * H, CM), wr[...])
        side = dot_nt(pg[pl.ds(k * 4 * Q, 4 * Q), :], wp[...])
        for half in range(2):
            ob[half] = main[:, half * CM : (half + 1) * CM].reshape(8, H, CM)
            for m in range(4):
                ob[half, 2 * m, pl.ds(0, Q, stride=2), :] += side[m * Q : (m + 1) * Q, half * CM : (half + 1) * CM]
            img[pl.ds(k * 8, 8), :, half * CM : (half + 1) * CM] = ob[half].astype(BF16)
        image_out(k).start()

    loop(12, pass4)
    loop(12, lambda k: image_out(k).wait())

    def each(n, make):
        loop(n, lambda d: make(d + 1).start())
        loop(n, lambda d: make(d + 1).wait())

    def chunk(p):
        return pl.ds(pl.multiple_of(p * CHUNK, CHUNK), CHUNK)

    def piece(p):
        return pl.ds(pl.multiple_of(p * PIECE, PIECE), PIECE)

    ng = NR * NS

    def scatter1(d):
        peer = lax.rem(col + d, NC)
        return remote(s1.at[chunk(peer)], r1.at[col], sem1.at[0, d], sem1.at[1, d], {"col": peer})

    each(NC - 1, scatter1)
    r1[col] = s1[chunk(col), :]
    a1[...] = sum(r1[p].astype(F32) for p in range(NC))

    def scatter2(d):
        q = lax.rem(grp + d, ng)
        return remote(a1.at[piece(q)], r2.at[grp], sem2.at[0, d], sem2.at[1, d], grp_peer(d))

    each(ng - 1, scatter2)
    r2[grp] = a1[piece(grp), :]
    a3[piece(grp), :] = sum(r2[p] for p in range(ng)) * SCALE

    def gather3(d):
        return remote(a3.at[piece(grp)], a3.at[piece(grp)], sem3.at[0, d], sem3.at[1, d], grp_peer(d))

    each(ng - 1, gather3)
    s3[...] = a3[...].astype(BF16)
    r4[col] = s3[...]

    def gather4(d):
        return remote(s3, r4.at[col], sem4.at[0, d], sem4.at[1, d], col_peer(d))

    each(NC - 1, gather4)

    for p in range(NC):
        s5[p, 32:40, :] = jnp.zeros((8, CM), F32)
        if p < 5:
            s5[p, 32:33, :] = a_misc[p : p + 1, :]
    for half in range(2):
        t = a_wr[:, half * CM : (half + 1) * CM].T * SCALE
        for p in range(4):
            s5[half * 4 + p, 0:32, :] = t[p * 32 : (p + 1) * 32, :]

    def scatter5(d):
        peer = lax.rem(col + d, NC)
        return remote(s5.at[peer], r5.at[col], sem5.at[0, d], sem5.at[1, d], {"col": peer})

    each(NC - 1, scatter5)
    r5[col] = s5[col]
    a5[...] = sum(r5[p] for p in range(NC))
    r6[grp] = a5[...]

    def gather6(d):
        return remote(a5, r6.at[grp], sem6.at[0, d], sem6.at[1, d], grp_peer(d))

    each(ng - 1, gather6)
    a5[...] = sum(r6[p] for p in range(ng))
    r7[col] = a5[...]

    def gather7(d):
        return remote(a5, r7.at[col], sem7.at[0, d], sem7.at[1, d], col_peer(d))

    each(NC - 1, gather7)

    for p in range(3):
        o_spatial[p * CHUNK : (p + 1) * CHUNK, :] = r4[p].astype(F32)

    def summed(at, n):
        return r4[at // CHUNK, at % CHUNK : at % CHUNK + n, :].astype(F32)

    for q in range(4):
        o_expand[:, q * CM : (q + 1) * CM] = summed(1152 + q * 128, 128)
        for part in range(2):
            o_project[part * 128 : (part + 1) * 128, q * CM : (q + 1) * CM] = summed(1664 + q * 256 + part * 128, 128)
    for p in range(NC):
        o_reduce[p * 32 : (p + 1) * 32, :] = r7[p, 0:32, :]
    for k in range(4):
        column = jnp.sum(jnp.where(eye, r7[k, 32:33, :], 0.0), axis=1, keepdims=True)
        o_classify[k * CM : (k + 1) * CM, 0:1] = -column
        o_classify[k * CM : (k + 1) * CM, 1:2] = column
    o_loss[...] = r7[4, 32:33, 0:1]


def per_device(image, wr, ws, we, wp, wc, mask, label):
    vmem = pl.BlockSpec(memory_space=pltpu.VMEM)
    hbm = pl.BlockSpec(memory_space=pl.ANY)
    v = pltpu.VMEM
    dma = pltpu.SemaphoreType.DMA
    scratch = [
        v((H, H, CI), BF16),
        v((H, H, CM), F32),
        v((8, 8 + H, CM), F32),
        v((Q + 1, Q, 3 * CM), BF16),
        v((Q, Q, 3 * CM), BF16),
        v((Q, Q, CI), BF16),
        v((2, H, CM), F32),
        v((H, CM), F32),
        v((H, CM), BF16),
        v((H, CM), BF16),
        v((16, CM), BF16),
        v((H + 16, CM), F32),
        v((Q, 3 * CM), BF16),
        v((TB * Q, CM), F32),
        v((TB * Q, CM), BF16),
        v((TB * Q, CO), F32),
        v((TB * Q, CO), F32),
        v((2, TB * Q, CM), F32),
        v((3, 8, CO), F32),
        v((8, CO), F32),
        v((TB * Q, CO), BF16),
        v((Q * Q, CO), BF16),
        v((8, Q + 8, CM), F32),
        v((Q + 1, Q, 2 * CM), BF16),
        v((3, 2 * CM, 2 * CM), BF16),
        v((2, 8, Q, 2 * CM), F32),
        v((2, H, CM), F32),
        v((H, H, CM), BF16),
        v((Q, CM), BF16),
        v((16, CM), BF16),
        v((Q + 16, CM), F32),
        v((Q, 2 * CM), BF16),
        v((Q, CM), F32),
        v((2, 8, H, CM), F32),
        v((CM, 9 * CM), F32),
        v((CM, CO), F32),
        v((CI, CO), F32),
        v((CM, CI), F32),
        v((8, CM), F32),
        v((NC * CHUNK, CM), BF16),
        v((NC, CHUNK, CM), BF16),
        v((CHUNK, CM), F32),
        v((NR * NS, PIECE, CM), F32),
        v((CHUNK, CM), F32),
        v((CHUNK, CM), BF16),
        v((NC, CHUNK, CM), BF16),
        v((NC, 40, CM), F32),
        v((NC, 40, CM), F32),
        v((40, CM), F32),
        v((NR * NS, 40, CM), F32),
        v((NC, 40, CM), F32),
        dma((IMG_CHUNKS,)),
        dma((12,)),
        dma((6,)),
        dma((6,)),
        dma((2, NC)),
        dma((2, NR * NS)),
        dma((2, NR * NS)),
        dma((2, NC)),
        dma((2, NC)),
        dma((2, NR * NS)),
        dma((2, NC)),
    ]
    shapes = [image.shape, (CI, CM), (9 * CM, CM), (CM, CO), (CI, CO), (CO, 2), (1, 1)]
    out = pl.pallas_call(
        kernel,
        out_shape=[jax.ShapeDtypeStruct(s, BF16 if k == 0 else F32) for k, s in enumerate(shapes)],
        in_specs=[hbm] + [vmem] * 6 + [pl.BlockSpec(memory_space=pltpu.SMEM)],
        out_specs=[hbm] + [vmem] * 6,
        scratch_shapes=scratch,
        compiler_params=pltpu.CompilerParams(
            collective_id=0, has_side_effects=True, vmem_limit_bytes=56 * 1024 * 1024
        ),
        cost_estimate=pl.CostEstimate(flops=7_000_000_000, bytes_accessed=12_000_000, transcendentals=4_000_000),
    )(image, wr, ws.reshape(3, 3 * CM, CM), we, wp, wc, mask[0], label)
    grad_image, g_reduce, g_spatial, g_expand, g_project, g_classify, loss = out
    return grad_image, g_reduce, g_spatial.reshape(3, 3, CM, CM), g_expand, g_project, g_classify, loss[0, 0]


def solution(mesh):
    in_specs = (P("slide", "row", "col", None), P(), P(), P(), P(), P(), P("slide", None, None), P("slide"))
    out_specs = (P("slide", "row", "col", None), P(), P(), P(), P(), P(), P())
    return jax.shard_map(per_device, mesh=mesh, in_specs=in_specs, out_specs=out_specs, check_vma=False)
```

```python
import jax
import jax.numpy as jnp
from jax import lax
from jax.experimental import pallas as pl
from jax.experimental.pallas import tpu as pltpu
from jax.sharding import PartitionSpec as P

EPSILON = 1e-05
MESH = pl.DeviceIdType.MESH
F32 = jnp.float32
BF16 = jnp.bfloat16

NR, NC, NS = 4, 8, 4
H = 96
Q = 48
CI, CM, CO = 256, 128, 512
TB = 16
SCALE = 1.0 / 288.0
CHUNK = 384
PIECE = CHUNK // (NR * NS)
IMG_CHUNKS = 12


def dot(a, b):
    return lax.dot_general(a, b, (((1,), (0,)), ((), ())), preferred_element_type=F32)


def dot_nt(a, b):
    return lax.dot_general(a, b, (((1,), (1,)), ((), ())), preferred_element_type=F32)


def dot_tn(a, b):
    return lax.dot_general(a, b, (((0,), (0,)), ((), ())), preferred_element_type=F32)


def lane_mean(x, ones):
    return dot(x.astype(BF16), ones)


def rms_scale(v, ones):
    return lax.rsqrt(lane_mean(v * v, ones) + EPSILON)


def act(v, ones):
    half = v * (0.5 * rms_scale(v, ones))
    return half * jnp.tanh(half) + half


def silu_slope(half):
    t = jnp.tanh(half)
    return (0.5 + 0.5 * t) * (1.0 + half * (1.0 - t))


def act_vjp(v, g, ones):
    r = rms_scale(v, ones)
    n = v * r
    dn = g * silu_slope(0.5 * n)
    return r * (dn - n * lane_mean(dn * n, ones))


def lanes(k):
    return slice(k * CM, (k + 1) * CM)


def loop(n, body):
    def step(i, carry):
        body(i)
        return carry

    lax.fori_loop(0, n, step, 0)


def kernel(
    img_hbm, wr, ws, we, wp, wc, mask, label,
    gimg_hbm, o_reduce, o_spatial, o_expand, o_project, o_classify, o_loss,
    img, pre, actb, rc_odd, rc_even, evp, evb, colb, col16, hcol, hcor, hcolf, srow,
    psp, spat, ne, npj, r_e, r_p, feat, gb, dnb, eg, pg, dbuf, dcat, wback, eo, natb, prg16,
    dright, dcor, drightf, drow, dcol, ob,
    a_ws, a_we, a_wp, a_wr, a_misc,
    s1, r1, a1, r2, a3, s3, r4, s5, r5, a5, r6, a7, r7,
    sem_in, sem_out, sem_h, sem_g, sem1, sem2, sem3, sem4, sem5, sem6, sem7,
):
    row, col, sld = lax.axis_index("row"), lax.axis_index("col"), lax.axis_index("slide")
    grp = row * NS + sld
    has_up, has_down = row > 0, row < NR - 1
    has_left, has_right = col > 0, col < NC - 1

    rows_in = H // IMG_CHUNKS

    def image_copy(k):
        return pltpu.make_async_copy(
            img_hbm.at[0, pl.ds(k * rows_in, rows_in)], img.at[pl.ds(k * rows_in, rows_in)], sem_in.at[k]
        )

    loop(IMG_CHUNKS, lambda k: image_copy(k).start())

    def col_peer(d):
        return {"col": lax.rem(col + d, NC)}

    def grp_peer(d):
        q = lax.rem(grp + d, NR * NS)
        return {"row": q // NS, "slide": lax.rem(q, NS)}

    barrier = pltpu.get_barrier_semaphore()
    loop(NC - 1, lambda d: pl.semaphore_signal(barrier, inc=1, device_id=col_peer(d + 1), device_id_type=MESH))
    loop(NR * NS - 1, lambda d: pl.semaphore_signal(barrier, inc=1, device_id=grp_peer(d + 1), device_id_type=MESH))
    to_diag = has_down & has_right
    from_diag = has_up & has_left

    @pl.when(to_diag)
    def _():
        pl.semaphore_signal(barrier, inc=1, device_id={"row": row + 1, "col": col + 1}, device_id_type=MESH)

    @pl.when(from_diag)
    def _():
        pl.semaphore_signal(barrier, inc=1, device_id={"row": row - 1, "col": col - 1}, device_id_type=MESH)

    wback[...] = jnp.zeros_like(wback)

    def tap(a, b):
        return ws[a, b * CM : (b + 1) * CM, :]

    for slot, a in ((0, 1), (1, 2), (2, 0)):
        wback[slot, 0:CM, 0:CM] = tap(a, 1)
        wback[slot, CM : 2 * CM, 0:CM] = tap(a, 2)
        wback[slot, CM : 2 * CM, CM : 2 * CM] = tap(a, 0)
    actb[:, 0:8, :] = jnp.zeros_like(actb[:, 0:8, :])
    dbuf[:, Q : Q + 8, :] = jnp.zeros_like(dbuf[:, Q : Q + 8, :])
    ones_m = jnp.full((CM, CM), 1.0 / CM, BF16)
    ones_o = jnp.full((CM, CM), 1.0 / CO, BF16)
    a_ws[...] = jnp.zeros_like(a_ws)
    a_we[...] = jnp.zeros_like(a_we)
    a_wp[...] = jnp.zeros_like(a_wp)
    a_wr[...] = jnp.zeros_like(a_wr)
    a_misc[...] = jnp.zeros_like(a_misc)

    @pl.when(jnp.logical_not(has_up))
    def _():
        rc_odd[0] = jnp.zeros_like(rc_odd[0])

    @pl.when(jnp.logical_not(has_left))
    def _():
        hcol[...] = jnp.zeros_like(hcol)

    @pl.when(jnp.logical_not(from_diag))
    def _():
        hcor[...] = jnp.zeros_like(hcor)

    @pl.when(jnp.logical_not(has_down))
    def _():
        dcat[Q] = jnp.zeros_like(dcat[Q])

    @pl.when(jnp.logical_not(has_right))
    def _():
        dright[...] = jnp.zeros_like(dright)

    @pl.when(jnp.logical_not(to_diag))
    def _():
        dcor[...] = jnp.zeros_like(dcor)

    drow_w = wc[1:2, :] - wc[0:1, :]
    sign = 1.0 - 2.0 * label[0].astype(F32)
    tissue_all = mask[...].astype(F32)
    tiles = jnp.sum(jnp.sum(tissue_all, axis=0), axis=1, keepdims=True)
    mask_r = lax.broadcasted_iota(jnp.int32, mask.shape, 0)
    mask_c = lax.broadcasted_iota(jnp.int32, mask.shape, 2)

    def pass1(k):
        image_copy(k).wait()
        x = img[pl.ds(k * 8, 8)].reshape(8 * H, CI)
        v = dot(x, wr[...])
        pre[pl.ds(k * 8, 8)] = v.reshape(8, H, CM)
        actb[:, 8 : 8 + H, :] = act(v, ones_m).reshape(8, H, CM)
        for r in range(8):
            rows, at = (rc_even, k * 4 + r // 2) if r % 2 == 0 else (rc_odd, k * 4 + r // 2 + 1)
            for b in range(3):
                rows[at, :, b * CM : (b + 1) * CM] = actb[r, pl.ds(7 + b, Q, stride=2), :].astype(BF16)
            colb[pl.ds(k * 8 + r, 1), :] = actb[r, 7 + H : 8 + H, :]

    loop(IMG_CHUNKS, pass1)

    col16[...] = colb[...].astype(BF16)
    srow[...] = rc_odd[Q]

    def remote(src, dst, send, recv, device):
        return pltpu.make_async_remote_copy(
            src_ref=src, dst_ref=dst, send_sem=send, recv_sem=recv, device_id=device, device_id_type=MESH
        )

    down = remote(srow, rc_odd.at[0], sem_h.at[0], sem_h.at[1], {"row": lax.rem(row + 1, NR)})
    right = remote(col16, hcol, sem_h.at[2], sem_h.at[3], {"col": lax.rem(col + 1, NC)})
    diag = remote(
        col16.at[pl.ds(H - 16, 16)], hcor, sem_h.at[4], sem_h.at[5],
        {"row": lax.rem(row + 1, NR), "col": lax.rem(col + 1, NC)},
    )
    n_diag = jnp.where(to_diag, 1, 0) + jnp.where(from_diag, 1, 0)
    pl.semaphore_wait(barrier, NC - 1 + NR * NS - 1 + n_diag)
    forward = ((down, has_down, has_up), (right, has_right, has_left), (diag, to_diag, from_diag))
    for copy, sends, _ in forward:
        pl.when(sends)(copy.start)

    def even_rows(m):
        x = img[2 * m].astype(F32)
        for half in range(2):
            evb[half] = x[:, half * CM : (half + 1) * CM]
        for half in range(2):
            evp[m, :, half * CM : (half + 1) * CM] = evb[half, pl.ds(0, Q, stride=2), :].astype(BF16)

    loop(Q, even_rows)

    def project(b):
        at = pl.ds(b * 8 * Q, 8 * Q)
        p = dot(evp[pl.ds(b * 8, 8)].reshape(8 * Q, CI), wp[...])
        npj[at, :] = p
        r_p[at, :] = lax.rsqrt(lane_mean(sum(p[:, lanes(k)] * p[:, lanes(k)] for k in range(4)), ones_o) + EPSILON)

    loop(6, project)

    for copy, sends, takes in forward:
        pl.when(takes)(copy.wait_recv)
        pl.when(sends)(copy.wait_send)

    hcolf[0:H] = hcol[...].astype(F32)
    hcolf[H : H + 16] = hcor[...].astype(F32)
    first = lax.broadcasted_iota(jnp.int32, (16, CM), 0) == 0

    def patch_left(rows, at, value):
        old = rows[at, 0:16, 0:CM].astype(F32)
        rows[at, 0:16, 0:CM] = jnp.where(first, value, old).astype(BF16)

    patch_left(rc_odd, 0, hcolf[H + 15 : H + 16, :])

    def patch_rows(m):
        patch_left(rc_even, m, hcolf[pl.ds(2 * m, 1), :])
        patch_left(rc_odd, m + 1, hcolf[pl.ds(2 * m + 1, 1), :])

    loop(Q, patch_rows)

    npx = TB * Q

    def taps(a, at, n):
        if a == 1:
            return rc_even[pl.ds(at, n)].reshape(n * Q, 3 * CM)
        return rc_odd[pl.ds(at + a // 2, n)].reshape(n * Q, 3 * CM)

    def tile_row(u):
        i0 = u * TB

        def convolve(b):
            at = i0 + b * 8
            v = sum(dot(taps(a, at, 8), ws[a]) for a in range(3))
            psp[pl.ds(b * 8 * Q, 8 * Q), :] = v
            spat[pl.ds(b * 8 * Q, 8 * Q), :] = act(v, ones_m).astype(BF16)

        loop(2, convolve)

        def expand(b):
            at = pl.ds(b * 8 * Q, 8 * Q)
            e = dot(spat[at, :], we[...])
            ne[at, :] = e
            r_e[at, :] = lax.rsqrt(lane_mean(sum(e[:, lanes(k)] * e[:, lanes(k)] for k in range(4)), ones_o) + EPSILON)

        loop(2, expand)
        feat[...] = jnp.zeros_like(feat)

        def merge(b):
            at = pl.ds(b * 4 * Q, 4 * Q)
            out = pl.ds(i0 * Q + b * 4 * Q, 4 * Q)
            h_e, h_p = 0.5 * r_e[at, :], 0.5 * r_p[out, :]
            for k in range(4):
                half = ne[at, lanes(k)] * h_e + npj[out, lanes(k)] * h_p
                merged = half * jnp.tanh(half) + half
                feat[:, lanes(k)] += jnp.sum(merged.reshape(4, Q, CM), axis=0)

        loop(4, merge)

        for v in range(3):
            f = jnp.sum(feat[v * TB : (v + 1) * TB, :], axis=0, keepdims=True) * (1.0 / (TB * TB))
            margin = jnp.sum(f * drow_w, axis=1, keepdims=True) * sign
            here = (mask_r == row * 3 + u) & (mask_c == col * 3 + v)
            tissue = jnp.where(here, tissue_all, 0.0)
            tissue = jnp.sum(jnp.sum(tissue, axis=0), axis=1, keepdims=True)
            soft = jnp.maximum(margin, 0.0) + jnp.log(1.0 + jnp.exp(-jnp.abs(margin)))
            weight = tissue * (0.5 + 0.5 * jnp.tanh(0.5 * margin)) / tiles * sign
            for k in range(CO // CM):
                a_misc[k : k + 1, :] += f[:, k * CM : (k + 1) * CM] * weight
            a_misc[4:5, :] += jnp.broadcast_to(tissue * soft / tiles, (1, CM))
            gb[v * TB : (v + 1) * TB, :] = jnp.broadcast_to(drow_w * (weight * 288.0), (TB, CO))

        def unmerge(b):
            at = pl.ds(b * 4 * Q, 4 * Q)
            out = pl.ds(i0 * Q + b * 4 * Q, 4 * Q)
            s_e, s_p = r_e[at, :], r_p[out, :]
            z_e, z_p = 0.0, 0.0
            for k in range(4):
                n_e, n_p = ne[at, lanes(k)] * s_e, npj[out, lanes(k)] * s_p
                slope = silu_slope(0.5 * (n_e + n_p)).reshape(4, Q, CM)
                dn = (slope * gb[:, lanes(k)][None]).reshape(4 * Q, CM)
                dnb[:, lanes(k)] = dn
                z_e, z_p = z_e + dn * n_e, z_p + dn * n_p
            m_e, m_p = lane_mean(z_e, ones_o), lane_mean(z_p, ones_o)
            for k in range(4):
                dn = dnb[:, lanes(k)]
                n_e, n_p = ne[at, lanes(k)] * s_e, npj[out, lanes(k)] * s_p
                eg[at, lanes(k)] = (s_e * (dn - n_e * m_e)).astype(BF16)
                pg[out, lanes(k)] = (s_p * (dn - n_p * m_p)).astype(BF16)

        loop(4, unmerge)

        a_we[...] += dot_tn(spat[...], eg[...])
        a_wp[...] += dot_tn(evp[pl.ds(i0, TB)].reshape(npx, CI), pg[pl.ds(i0 * Q, npx), :])

        def unconvolve(b):
            at = pl.ds(b * 8 * Q, 8 * Q)
            g = dot_nt(eg[at, :], we[...])
            d = act_vjp(psp[at, :], g, ones_m)
            dbuf[:, 0:Q, :] = d.reshape(8, Q, CM)
            d16 = d.astype(BF16)
            dcat[pl.ds(i0 + b * 8, 8), :, 0:CM] = d16.reshape(8, Q, CM)
            for r in range(8):
                dcat[i0 + b * 8 + r, :, CM : 2 * CM] = dbuf[r, 1 : Q + 1, :].astype(BF16)
                dcol[pl.ds(i0 + b * 8 + r, 1), :] = dbuf[r, 0:1, :]

        loop(2, unconvolve)

    loop(3, tile_row)

    drow[...] = dcat[0]
    col16[0:Q] = dcol[...].astype(BF16)
    up = remote(drow, dcat.at[Q], sem_g.at[0], sem_g.at[1], {"row": lax.rem(row + NR - 1, NR)})
    left = remote(col16.at[pl.ds(0, Q)], dright, sem_g.at[2], sem_g.at[3], {"col": lax.rem(col + NC - 1, NC)})
    gaid = remote(
        col16.at[pl.ds(0, 16)], dcor, sem_g.at[4], sem_g.at[5],
        {"row": lax.rem(row + NR - 1, NR), "col": lax.rem(col + NC - 1, NC)},
    )
    backward = ((up, has_up, has_down), (left, has_left, has_right), (gaid, from_diag, to_diag))
    for copy, sends, _ in backward:
        pl.when(sends)(copy.start)

    def spatial_weight_grad(u):
        d16 = dcat[pl.ds(u * TB, TB), :, 0:CM].reshape(npx, CM)
        for a in range(3):
            a_ws[:, a * 3 * CM : (a + 1) * 3 * CM] += dot_tn(d16, taps(a, u * TB, TB))

    loop(3, spatial_weight_grad)

    for t in range(9):
        s1[t * CM : (t + 1) * CM, :] = a_ws[:, t * CM : (t + 1) * CM].T.astype(BF16)
    for q in range(4):
        s1[1152 + q * 128 : 1152 + (q + 1) * 128, :] = a_we[:, q * CM : (q + 1) * CM].astype(BF16)
        s1[1664 + q * 256 : 1664 + (q + 1) * 256, :] = a_wp[:, q * CM : (q + 1) * CM].astype(BF16)
    s1[2688:3072, :] = jnp.zeros((384, CM), BF16)

    ng = NR * NS

    def start(n, make):
        loop(n, lambda d: make(d + 1).start())

    def finish(n, make):
        loop(n, lambda d: make(d + 1).wait())

    def chunk(p):
        return pl.ds(pl.multiple_of(p * CHUNK, CHUNK), CHUNK)

    def piece(p):
        return pl.ds(pl.multiple_of(p * PIECE, PIECE), PIECE)

    def scatter1(d):
        peer = lax.rem(col + d, NC)
        return remote(s1.at[chunk(peer)], r1.at[col], sem1.at[0, d], sem1.at[1, d], {"col": peer})

    def scatter2(d):
        q = lax.rem(grp + d, ng)
        return remote(a1.at[piece(q)], r2.at[grp], sem2.at[0, d], sem2.at[1, d], grp_peer(d))

    def gather3(d):
        return remote(a3.at[piece(grp)], a3.at[piece(grp)], sem3.at[0, d], sem3.at[1, d], grp_peer(d))

    def gather4(d):
        return remote(s3, r4.at[col], sem4.at[0, d], sem4.at[1, d], col_peer(d))

    def scatter5(d):
        peer = lax.rem(col + d, NC)
        return remote(s5.at[peer], r5.at[col], sem5.at[0, d], sem5.at[1, d], {"col": peer})

    def gather6(d):
        return remote(a5, r6.at[grp], sem6.at[0, d], sem6.at[1, d], grp_peer(d))

    def gather7(d):
        return remote(a7, r7.at[col], sem7.at[0, d], sem7.at[1, d], col_peer(d))

    start(NC - 1, scatter1)

    for copy, sends, takes in backward:
        pl.when(takes)(copy.wait_recv)
        pl.when(sends)(copy.wait_send)

    drightf[0:Q] = dright[...].astype(F32)
    drightf[Q : Q + 16] = dcor[...].astype(F32)
    last = lax.broadcasted_iota(jnp.int32, (16, CM), 0) == 15

    def patch_right(at, value):
        old = dcat[at, Q - 16 : Q, CM : 2 * CM].astype(F32)
        dcat[at, Q - 16 : Q, CM : 2 * CM] = jnp.where(last, value, old).astype(BF16)

    loop(Q, lambda m: patch_right(m, drightf[pl.ds(m, 1), :]))
    patch_right(Q, drightf[Q : Q + 1, :])

    def pass3(b):
        i0 = b * 8
        here = dcat[pl.ds(i0, 8)].reshape(8 * Q, 2 * CM)
        below = dcat[pl.ds(i0 + 1, 8)].reshape(8 * Q, 2 * CM)
        eo[0] = dot_nt(here, wback[0]).reshape(8, Q, 2 * CM)
        eo[1] = (dot_nt(here, wback[1]) + dot_nt(below, wback[2])).reshape(8, Q, 2 * CM)

        def some_rows(c):
            for rp in range(2):
                at = 2 * (i0 + 4 * c)
                for cp in range(2):
                    v = jnp.concatenate([pre[at + 2 * i + rp, pl.ds(cp, Q, stride=2), :] for i in range(4)], axis=0)
                    g = eo[rp, pl.ds(4 * c, 4), :, lanes(cp)].reshape(4 * Q, CM)
                    d = act_vjp(v, g, ones_m)
                    for i in range(4):
                        natb[rp, i, pl.ds(cp, Q, stride=2), :] = d[i * Q : (i + 1) * Q]
                for i in range(4):
                    prg16[at + 2 * i + rp] = natb[rp, i].astype(BF16)

        loop(2, some_rows)
        rows = pl.ds(2 * i0, 16)
        a_wr[...] += dot_tn(prg16[rows].reshape(16 * H, CM), img[rows].reshape(16 * H, CI))

    loop(6, pass3)

    finish(NC - 1, scatter1)
    r1[col] = s1[chunk(col), :]
    a1[...] = sum(r1[p].astype(F32) for p in range(NC))
    start(ng - 1, scatter2)

    for p in range(NC):
        s5[p, 32:40, :] = jnp.zeros((8, CM), F32)
        if p < 5:
            s5[p, 32:33, :] = a_misc[p : p + 1, :]
    for half in range(2):
        t = a_wr[:, lanes(half)].T * SCALE
        for p in range(4):
            s5[half * 4 + p, 0:32, :] = t[p * 32 : (p + 1) * 32, :]
    start(NC - 1, scatter5)

    def image_out(k):
        rows = pl.ds(k * 8, 8)
        return pltpu.make_async_copy(img.at[rows], gimg_hbm.at[0, rows], sem_out.at[k])

    def pass4(k):
        main = dot_nt(prg16[pl.ds(k * 8, 8)].reshape(8 * H, CM), wr[...])
        side = dot_nt(pg[pl.ds(k * 4 * Q, 4 * Q), :], wp[...])
        for m in range(4):
            at = k * 8 + 2 * m
            for half in range(2):
                ob[half, m] = main[2 * m * H : (2 * m + 1) * H, lanes(half)]
                ob[half, m, pl.ds(0, Q, stride=2), :] += side[m * Q : (m + 1) * Q, lanes(half)]
                gimg_hbm[0, at, :, lanes(half)] = ob[half, m].astype(BF16)
            gimg_hbm[0, at + 1] = main[(2 * m + 1) * H : (2 * m + 2) * H].astype(BF16)

    def some(lo, hi):
        loop(hi - lo, lambda k: pass4(lo + k))

    some(0, 4)
    finish(ng - 1, scatter2)
    r2[grp] = a1[piece(grp), :]
    a3[piece(grp), :] = sum(r2[p] for p in range(ng)) * SCALE
    start(ng - 1, gather3)
    finish(NC - 1, scatter5)
    r5[col] = s5[col]
    a5[...] = sum(r5[p] for p in range(NC))
    r6[grp] = a5[...]
    start(ng - 1, gather6)
    some(4, 8)
    finish(ng - 1, gather3)
    s3[...] = a3[...].astype(BF16)
    r4[col] = s3[...]
    start(NC - 1, gather4)
    finish(ng - 1, gather6)
    a7[...] = sum(r6[p] for p in range(ng))
    r7[col] = a7[...]
    start(NC - 1, gather7)
    some(8, 12)
    finish(NC - 1, gather4)
    finish(NC - 1, gather7)

    for p in range(3):
        o_spatial[p * CHUNK : (p + 1) * CHUNK, :] = r4[p].astype(F32)

    def summed(at, n):
        return r4[at // CHUNK, at % CHUNK : at % CHUNK + n, :].astype(F32)

    for q in range(4):
        o_expand[:, q * CM : (q + 1) * CM] = summed(1152 + q * 128, 128)
        for part in range(2):
            o_project[part * 128 : (part + 1) * 128, q * CM : (q + 1) * CM] = summed(1664 + q * 256 + part * 128, 128)
    for p in range(NC):
        o_reduce[p * 32 : (p + 1) * 32, :] = r7[p, 0:32, :]
    for k in range(4):
        o_classify[0:1, lanes(k)] = -r7[k, 32:33, :]
        o_classify[1:2, lanes(k)] = r7[k, 32:33, :]
    o_loss[...] = r7[4, 32:33, 0:1]


def hand_over(*refs):
    n = (len(refs) - 1) // 2
    given, taken, sem = refs[:n], refs[n : 2 * n], refs[-1]
    copies = [pltpu.make_async_copy(a, b, sem.at[k]) for k, (a, b) in enumerate(zip(given, taken))]
    for c in copies:
        c.start()
    for c in copies:
        c.wait()


def per_device(image, wr, ws, we, wp, wc, mask, label):
    vmem = pl.BlockSpec(memory_space=pltpu.VMEM)
    hbm = pl.BlockSpec(memory_space=pl.ANY)
    v = pltpu.VMEM
    dma = pltpu.SemaphoreType.DMA
    scratch = [
        v((H, H, CI), BF16),
        v((H, H, CM), F32),
        v((8, 8 + H, CM), F32),
        v((Q + 1, Q, 3 * CM), BF16),
        v((Q, Q, 3 * CM), BF16),
        v((Q, Q, CI), BF16),
        v((2, H, CM), F32),
        v((H, CM), F32),
        v((H, CM), BF16),
        v((H, CM), BF16),
        v((16, CM), BF16),
        v((H + 16, CM), F32),
        v((Q, 3 * CM), BF16),
        v((TB * Q, CM), F32),
        v((TB * Q, CM), BF16),
        v((TB * Q, CO), F32),
        v((Q * Q, CO), F32),
        v((TB * Q, CM), F32),
        v((Q * Q, CM), F32),
        v((Q, CO), F32),
        v((Q, CO), F32),
        v((4 * Q, CO), F32),
        v((TB * Q, CO), BF16),
        v((Q * Q, CO), BF16),
        v((8, Q + 8, CM), F32),
        v((Q + 1, Q, 2 * CM), BF16),
        v((3, 2 * CM, 2 * CM), BF16),
        v((2, 8, Q, 2 * CM), F32),
        v((2, 4, H, CM), F32),
        v((H, H, CM), BF16),
        v((Q, CM), BF16),
        v((16, CM), BF16),
        v((Q + 16, CM), F32),
        v((Q, 2 * CM), BF16),
        v((Q, CM), F32),
        v((2, 4, H, CM), F32),
        v((CM, 9 * CM), F32),
        v((CM, CO), F32),
        v((CI, CO), F32),
        v((CM, CI), F32),
        v((8, CM), F32),
        v((NC * CHUNK, CM), BF16),
        v((NC, CHUNK, CM), BF16),
        v((CHUNK, CM), F32),
        v((NR * NS, PIECE, CM), F32),
        v((CHUNK, CM), F32),
        v((CHUNK, CM), BF16),
        v((NC, CHUNK, CM), BF16),
        v((NC, 40, CM), F32),
        v((NC, 40, CM), F32),
        v((40, CM), F32),
        v((NR * NS, 40, CM), F32),
        v((40, CM), F32),
        v((NC, 40, CM), F32),
        dma((IMG_CHUNKS,)),
        dma((12,)),
        dma((6,)),
        dma((6,)),
        dma((2, NC)),
        dma((2, NR * NS)),
        dma((2, NR * NS)),
        dma((2, NC)),
        dma((2, NC)),
        dma((2, NR * NS)),
        dma((2, NC)),
    ]
    shapes = [image.shape, (CI, CM), (9 * CM, CM), (CM, CO), (CI, CO), (2, CO), (1, 1)]
    out = pl.pallas_call(
        kernel,
        out_shape=[v(s, BF16 if k == 0 else F32) for k, s in enumerate(shapes)],
        in_specs=[hbm] + [vmem] * 6 + [pl.BlockSpec(memory_space=pltpu.SMEM)],
        out_specs=[vmem] * 7,
        scratch_shapes=scratch,
        compiler_params=pltpu.CompilerParams(
            collective_id=0, has_side_effects=True, vmem_limit_bytes=50 * 1024 * 1024
        ),
        cost_estimate=pl.CostEstimate(flops=7_000_000_000, bytes_accessed=12_000_000, transcendentals=4_000_000),
    )(image, wr, ws.reshape(3, 3 * CM, CM), we, wp, wc.T, jnp.transpose(mask, (1, 0, 2)), label)
    out = pl.pallas_call(
        hand_over,
        out_shape=[jax.ShapeDtypeStruct(o.shape, o.dtype) for o in out],
        in_specs=[vmem] * len(out),
        out_specs=[hbm] * len(out),
        scratch_shapes=[dma((len(out),))],
        compiler_params=pltpu.CompilerParams(vmem_limit_bytes=1024 * 1024),
    )(*out)
    grad_image, g_reduce, g_spatial, g_expand, g_project, g_classify, loss = out
    return grad_image, g_reduce, g_spatial.reshape(3, 3, CM, CM), g_expand, g_project, g_classify.T, loss[0, 0]


def solution(mesh):
    in_specs = (P("slide", "row", "col", None), P(), P(), P(), P(), P(), P("slide", None, None), P("slide"))
    out_specs = (P("slide", "row", "col", None), P(), P(), P(), P(), P(), P())
    return jax.shard_map(per_device, mesh=mesh, in_specs=in_specs, out_specs=out_specs, check_vma=False)
```

```python
import jax
import jax.numpy as jnp
from jax import lax
from jax.experimental import pallas as pl
from jax.experimental.pallas import tpu as pltpu
from jax.sharding import PartitionSpec as P

EPSILON = 1e-05
MESH = pl.DeviceIdType.MESH
F32 = jnp.float32
BF16 = jnp.bfloat16

NR, NC, NS = 4, 8, 4
H = 96
Q = 48
CI, CM, CO = 256, 128, 512
TB = 16
SCALE = 1.0 / 288.0
CHUNK = 384
PIECE = CHUNK // (NR * NS)
IMG_CHUNKS = 12


def dot(a, b):
    return lax.dot_general(a, b, (((1,), (0,)), ((), ())), preferred_element_type=F32)


def dot_nt(a, b):
    return lax.dot_general(a, b, (((1,), (1,)), ((), ())), preferred_element_type=F32)


def dot_tn(a, b):
    return lax.dot_general(a, b, (((0,), (0,)), ((), ())), preferred_element_type=F32)


def lane_mean(x, ones):
    return dot(x.astype(BF16), ones)


def half_scale(squares, ones):
    return lax.rsqrt(lane_mean(squares, ones) + 4.0 * EPSILON)


def silu_vjp(half, g):
    t = jnp.tanh(half)
    return g * (1.0 + t) * (1.0 + half * (1.0 - t))


def silu(half):
    return half * jnp.tanh(half) + half


def act_vjp(half, scale, g, ones):
    dn = silu_vjp(half, g)
    return scale * (dn - half * lane_mean(dn * half, ones))


def lanes(k):
    return slice(k * CM, (k + 1) * CM)


def loop(n, body):
    def step(i, carry):
        body(i)
        return carry

    lax.fori_loop(0, n, step, 0)


def unrolled(n, body):
    for i in range(n):
        body(i)


def kernel(
    img_hbm, wr_hbm, ws_hbm, we_hbm, wp_hbm, wc, mask, label,
    gimg_hbm, o_reduce, o_spatial, o_expand, o_project, o_classify, o_loss,
    wr, ws, we, wp, img, pre, prs, actb, rc_odd, rc_even, evp, evb, colb, col16, hcol, hcor, hcolf, srow,
    psp, spat, ne, npj, r_e, r_p, feat, gb, dnb, eg, pg, dbuf, dcat, wback, eo, natb, prg16,
    dright, dcor, drightf, drow, dcol, ob,
    a_ws, a_we, a_wp, a_wr, a_misc,
    s1, r0, r1, a1, r2, a3, s3, r4, s5, r5, a5, r6, a7, r7,
    sem_in, sem_w, sem_h, sem_g, sem0, sem1, sem2, sem3, sem4, sem5, sem6, sem7, sem8,
):
    row, col, sld = lax.axis_index("row"), lax.axis_index("col"), lax.axis_index("slide")
    grp = row * NS + sld
    has_up, has_down = row > 0, row < NR - 1
    has_left, has_right = col > 0, col < NC - 1

    rows_in = H // IMG_CHUNKS

    def image_copy(k):
        return pltpu.make_async_copy(
            img_hbm.at[0, pl.ds(k * rows_in, rows_in)], img.at[pl.ds(k * rows_in, rows_in)], sem_in.at[k]
        )

    weights = [
        pltpu.make_async_copy(a, b, sem_w.at[k])
        for k, (a, b) in enumerate(((wr_hbm, wr), (ws_hbm, ws), (we_hbm, we), (wp_hbm, wp)))
    ]
    weights[0].start()
    loop(IMG_CHUNKS, lambda k: image_copy(k).start())
    for copy in weights[1:]:
        copy.start()

    def col_peer(d):
        return {"col": lax.rem(col + d, NC)}

    def grp_peer(d):
        q = lax.rem(grp + d, NR * NS)
        return {"row": q // NS, "slide": lax.rem(q, NS)}

    barrier = pltpu.get_barrier_semaphore()
    loop(NC - 1, lambda d: pl.semaphore_signal(barrier, inc=1, device_id=col_peer(d + 1), device_id_type=MESH))
    loop(NR * NS - 1, lambda d: pl.semaphore_signal(barrier, inc=1, device_id=grp_peer(d + 1), device_id_type=MESH))
    to_diag = has_down & has_right
    from_diag = has_up & has_left

    @pl.when(to_diag)
    def _():
        pl.semaphore_signal(barrier, inc=1, device_id={"row": row + 1, "col": col + 1}, device_id_type=MESH)

    @pl.when(from_diag)
    def _():
        pl.semaphore_signal(barrier, inc=1, device_id={"row": row - 1, "col": col - 1}, device_id_type=MESH)

    actb[:, 0:8, :] = jnp.zeros_like(actb[:, 0:8, :])
    dbuf[:, Q : Q + 8, :] = jnp.zeros_like(dbuf[:, Q : Q + 8, :])
    ones_m = jnp.full((CM, CM), 4.0 / CM, BF16)
    ones_o = jnp.full((CM, CM), 4.0 / CO, BF16)
    a_ws[...] = jnp.zeros_like(a_ws)
    a_we[...] = jnp.zeros_like(a_we)
    a_wp[...] = jnp.zeros_like(a_wp)
    a_wr[...] = jnp.zeros_like(a_wr)
    a_misc[...] = jnp.zeros_like(a_misc)

    @pl.when(jnp.logical_not(has_up))
    def _():
        rc_odd[0] = jnp.zeros_like(rc_odd[0])

    @pl.when(jnp.logical_not(has_left))
    def _():
        hcol[...] = jnp.zeros_like(hcol)

    @pl.when(jnp.logical_not(from_diag))
    def _():
        hcor[...] = jnp.zeros_like(hcor)

    @pl.when(jnp.logical_not(has_down))
    def _():
        dcat[Q] = jnp.zeros_like(dcat[Q])

    @pl.when(jnp.logical_not(has_right))
    def _():
        dright[...] = jnp.zeros_like(dright)

    @pl.when(jnp.logical_not(to_diag))
    def _():
        dcor[...] = jnp.zeros_like(dcor)

    drow_w = wc[1:2, :] - wc[0:1, :]
    sign = 1.0 - 2.0 * label[0].astype(F32)
    tissue_all = mask[...].astype(F32)
    tiles = jnp.sum(jnp.sum(tissue_all, axis=0), axis=1, keepdims=True)
    mask_r = lax.broadcasted_iota(jnp.int32, mask.shape, 0)
    mask_c = lax.broadcasted_iota(jnp.int32, mask.shape, 2)

    weights[0].wait()

    def pass1(k):
        image_copy(k).wait()
        x = img[pl.ds(k * 8, 8)].reshape(8 * H, CI)
        v = dot(x, wr[...])
        scale = half_scale(v * v, ones_m)
        half = v * scale
        pre[pl.ds(k * 8, 8)] = half.reshape(8, H, CM)
        prs[pl.ds(k * 8, 8)] = scale.reshape(8, H, CM)
        actb[:, 8 : 8 + H, :] = silu(half).reshape(8, H, CM)
        for r in range(8):
            rows, at = (rc_even, k * 4 + r // 2) if r % 2 == 0 else (rc_odd, k * 4 + r // 2 + 1)
            for b in range(3):
                rows[at, :, b * CM : (b + 1) * CM] = actb[r, pl.ds(7 + b, Q, stride=2), :].astype(BF16)
            colb[pl.ds(k * 8 + r, 1), :] = actb[r, 7 + H : 8 + H, :]

    loop(IMG_CHUNKS, pass1)

    col16[...] = colb[...].astype(BF16)
    srow[...] = rc_odd[Q]

    def remote(src, dst, send, recv, device):
        return pltpu.make_async_remote_copy(
            src_ref=src, dst_ref=dst, send_sem=send, recv_sem=recv, device_id=device, device_id_type=MESH
        )

    down = remote(srow, rc_odd.at[0], sem_h.at[0], sem_h.at[1], {"row": lax.rem(row + 1, NR)})
    right = remote(col16, hcol, sem_h.at[2], sem_h.at[3], {"col": lax.rem(col + 1, NC)})
    diag = remote(
        col16.at[pl.ds(H - 16, 16)], hcor, sem_h.at[4], sem_h.at[5],
        {"row": lax.rem(row + 1, NR), "col": lax.rem(col + 1, NC)},
    )
    n_diag = jnp.where(to_diag, 1, 0) + jnp.where(from_diag, 1, 0)
    pl.semaphore_wait(barrier, NC - 1 + NR * NS - 1 + n_diag)
    forward = ((down, has_down, has_up), (right, has_right, has_left), (diag, to_diag, from_diag))
    for copy, sends, _ in forward:
        pl.when(sends)(copy.start)

    for copy in weights[1:]:
        copy.wait()
    wback[...] = jnp.zeros_like(wback)

    def tap(a, b):
        return ws[a, b * CM : (b + 1) * CM, :]

    for slot, a in ((0, 1), (1, 2), (2, 0)):
        wback[slot, 0:CM, 0:CM] = tap(a, 1)
        wback[slot, CM : 2 * CM, 0:CM] = tap(a, 2)
        wback[slot, CM : 2 * CM, CM : 2 * CM] = tap(a, 0)
    def even_rows(m):
        x = img[2 * m].astype(F32)
        for half in range(2):
            evb[half] = x[:, half * CM : (half + 1) * CM]
        for half in range(2):
            evp[m, :, half * CM : (half + 1) * CM] = evb[half, pl.ds(0, Q, stride=2), :].astype(BF16)

    loop(Q // 4, lambda m: unrolled(4, lambda i: even_rows(4 * m + i)))

    def project(b):
        at = pl.ds(b * 8 * Q, 8 * Q)
        p = dot(evp[pl.ds(b * 8, 8)].reshape(8 * Q, CI), wp[...])
        npj[at, :] = p
        r_p[at, :] = half_scale(sum(p[:, lanes(k)] * p[:, lanes(k)] for k in range(4)), ones_o)

    loop(3, lambda b: unrolled(2, lambda i: project(2 * b + i)))

    for copy, sends, takes in forward:
        pl.when(takes)(copy.wait_recv)
        pl.when(sends)(copy.wait_send)

    hcolf[0:H] = hcol[...].astype(F32)
    hcolf[H : H + 16] = hcor[...].astype(F32)
    first = lax.broadcasted_iota(jnp.int32, (16, CM), 0) == 0

    def patch_left(rows, at, value):
        old = rows[at, 0:16, 0:CM].astype(F32)
        rows[at, 0:16, 0:CM] = jnp.where(first, value, old).astype(BF16)

    patch_left(rc_odd, 0, hcolf[H + 15 : H + 16, :])

    def patch_rows(m):
        patch_left(rc_even, m, hcolf[pl.ds(2 * m, 1), :])
        patch_left(rc_odd, m + 1, hcolf[pl.ds(2 * m + 1, 1), :])

    loop(Q, patch_rows)

    npx = TB * Q

    def taps(a, at, n):
        if a == 1:
            return rc_even[pl.ds(at, n)].reshape(n * Q, 3 * CM)
        return rc_odd[pl.ds(at + a // 2, n)].reshape(n * Q, 3 * CM)

    def tile_row(u):
        i0 = u * TB

        def convolve(b):
            at = i0 + b * 8
            v = sum(dot(taps(a, at, 8), ws[a]) for a in range(3))
            scale = half_scale(v * v, ones_m)
            half = v * scale
            psp[0, pl.ds(b * 8 * Q, 8 * Q), :] = half
            psp[1, pl.ds(b * 8 * Q, 8 * Q), :] = scale
            spat[pl.ds(b * 8 * Q, 8 * Q), :] = silu(half).astype(BF16)

        unrolled(2, convolve)

        def expand(b):
            at = pl.ds(b * 8 * Q, 8 * Q)
            e = dot(spat[at, :], we[...])
            ne[at, :] = e
            r_e[at, :] = half_scale(sum(e[:, lanes(k)] * e[:, lanes(k)] for k in range(4)), ones_o)

        unrolled(2, expand)
        feat[...] = jnp.zeros_like(feat)

        def merge(b):
            at = pl.ds(b * 4 * Q, 4 * Q)
            out = pl.ds(i0 * Q + b * 4 * Q, 4 * Q)
            h_e, h_p = r_e[at, :], r_p[out, :]
            for k in range(4):
                half = ne[at, lanes(k)] * h_e + npj[out, lanes(k)] * h_p
                feat[:, lanes(k)] += jnp.sum(silu(half).reshape(4, Q, CM), axis=0)

        loop(4, merge)

        for v in range(3):
            f = jnp.sum(feat[v * TB : (v + 1) * TB, :], axis=0, keepdims=True) * (1.0 / (TB * TB))
            margin = jnp.sum(f * drow_w, axis=1, keepdims=True) * sign
            here = (mask_r == row * 3 + u) & (mask_c == col * 3 + v)
            tissue = jnp.where(here, tissue_all, 0.0)
            tissue = jnp.sum(jnp.sum(tissue, axis=0), axis=1, keepdims=True)
            soft = jnp.maximum(margin, 0.0) + jnp.log(1.0 + jnp.exp(-jnp.abs(margin)))
            weight = tissue * (0.5 + 0.5 * jnp.tanh(0.5 * margin)) / tiles * sign
            for k in range(CO // CM):
                a_misc[k : k + 1, :] += f[:, k * CM : (k + 1) * CM] * weight
            a_misc[4:5, :] += jnp.broadcast_to(tissue * soft / tiles, (1, CM))
            gb[v * TB : (v + 1) * TB, :] = jnp.broadcast_to(drow_w * (weight * 288.0), (TB, CO))

        def unmerge(b):
            at = pl.ds(b * 4 * Q, 4 * Q)
            out = pl.ds(i0 * Q + b * 4 * Q, 4 * Q)
            s_e, s_p = r_e[at, :], r_p[out, :]
            z_e, z_p = 0.0, 0.0
            for k in range(4):
                n_e, n_p = ne[at, lanes(k)] * s_e, npj[out, lanes(k)] * s_p
                dn = silu_vjp((n_e + n_p).reshape(4, Q, CM), gb[:, lanes(k)][None]).reshape(4 * Q, CM)
                dnb[:, lanes(k)] = dn
                z_e, z_p = z_e + dn * n_e, z_p + dn * n_p
            m_e, m_p = lane_mean(z_e, ones_o), lane_mean(z_p, ones_o)
            for k in range(4):
                dn = dnb[:, lanes(k)]
                n_e, n_p = ne[at, lanes(k)] * s_e, npj[out, lanes(k)] * s_p
                eg[at, lanes(k)] = (s_e * (dn - n_e * m_e)).astype(BF16)
                pg[out, lanes(k)] = (s_p * (dn - n_p * m_p)).astype(BF16)

        loop(4, unmerge)

        a_we[...] += dot_tn(spat[...], eg[...])
        a_wp[...] += dot_tn(evp[pl.ds(i0, TB)].reshape(npx, CI), pg[pl.ds(i0 * Q, npx), :])

        def unconvolve(b):
            at = pl.ds(b * 8 * Q, 8 * Q)
            g = dot_nt(eg[at, :], we[...])
            d = act_vjp(psp[0, at, :], psp[1, at, :], g, ones_m)
            dbuf[:, 0:Q, :] = d.reshape(8, Q, CM)
            d16 = d.astype(BF16)
            dcat[pl.ds(i0 + b * 8, 8), :, 0:CM] = d16.reshape(8, Q, CM)
            for r in range(8):
                dcat[i0 + b * 8 + r, :, CM : 2 * CM] = dbuf[r, 1 : Q + 1, :].astype(BF16)
                dcol[pl.ds(i0 + b * 8 + r, 1), :] = dbuf[r, 0:1, :]

        unrolled(2, unconvolve)

    loop(3, tile_row)

    drow[...] = dcat[0]
    col16[0:Q] = dcol[...].astype(BF16)
    up = remote(drow, dcat.at[Q], sem_g.at[0], sem_g.at[1], {"row": lax.rem(row + NR - 1, NR)})
    left = remote(col16.at[pl.ds(0, Q)], dright, sem_g.at[2], sem_g.at[3], {"col": lax.rem(col + NC - 1, NC)})
    gaid = remote(
        col16.at[pl.ds(0, 16)], dcor, sem_g.at[4], sem_g.at[5],
        {"row": lax.rem(row + NR - 1, NR), "col": lax.rem(col + NC - 1, NC)},
    )
    backward = ((up, has_up, has_down), (left, has_left, has_right), (gaid, from_diag, to_diag))
    for copy, sends, _ in backward:
        pl.when(sends)(copy.start)

    def spatial_weight_grad(u):
        d16 = dcat[pl.ds(u * TB, TB), :, 0:CM].reshape(npx, CM)
        for a in range(3):
            a_ws[:, a * 3 * CM : (a + 1) * 3 * CM] += dot_tn(d16, taps(a, u * TB, TB))

    loop(3, spatial_weight_grad)

    for t in range(9):
        s1[t * CM : (t + 1) * CM, :] = a_ws[:, t * CM : (t + 1) * CM].T.astype(BF16)
    for q in range(4):
        s1[1152 + q * 128 : 1152 + (q + 1) * 128, :] = a_we[:, q * CM : (q + 1) * CM].astype(BF16)
        s1[1664 + q * 256 : 1664 + (q + 1) * 256, :] = a_wp[:, q * CM : (q + 1) * CM].astype(BF16)
    s1[2688:3072, :] = jnp.zeros((384, CM), BF16)

    ng = NR * NS

    def start(n, make):
        loop(n, lambda d: make(d + 1).start())

    def finish(n, make):
        loop(n, lambda d: make(d + 1).wait())

    def chunk(p):
        return pl.ds(pl.multiple_of(p * CHUNK, CHUNK), CHUNK)

    def piece(p):
        return pl.ds(pl.multiple_of(p * PIECE, PIECE), PIECE)

    core, cy = lax.rem(col, 2), col // 2
    half_rows = NC // 2 * CHUNK

    def core_half(c):
        return pl.ds(pl.multiple_of(c * half_rows, half_rows), half_rows)

    def y_chunk(y):
        return chunk(core * (NC // 2) + y)

    other = {"col": col + 1 - 2 * core}

    def scatter0(d):
        return remote(s1.at[core_half(1 - core)], r0, sem0.at[0], sem0.at[1], other)

    def scatter1(d):
        peer = lax.rem(cy + d, NC // 2)
        return remote(s1.at[y_chunk(peer)], r1.at[cy], sem1.at[0, d], sem1.at[1, d], {"col": 2 * peer + core})

    def scatter2(d):
        q = lax.rem(grp + d, ng)
        return remote(a1.at[piece(q)], r2.at[grp], sem2.at[0, d], sem2.at[1, d], grp_peer(d))

    def gather3(d):
        return remote(a3.at[piece(grp)], a3.at[piece(grp)], sem3.at[0, d], sem3.at[1, d], grp_peer(d))

    def gather4(d):
        peer = lax.rem(cy + d, NC // 2)
        return remote(s3, r4.at[y_chunk(cy)], sem4.at[0, d], sem4.at[1, d], {"col": 2 * peer + core})

    def gather8(d):
        return remote(r4.at[core_half(core)], r4.at[core_half(core)], sem8.at[0], sem8.at[1], other)

    def scatter5(d):
        peer = lax.rem(col + d, NC)
        return remote(s5.at[peer], r5.at[col], sem5.at[0, d], sem5.at[1, d], {"col": peer})

    def gather6(d):
        return remote(a5, r6.at[grp], sem6.at[0, d], sem6.at[1, d], grp_peer(d))

    def gather7(d):
        return remote(a7, r7.at[col], sem7.at[0, d], sem7.at[1, d], col_peer(d))

    start(1, scatter0)

    finish(1, scatter0)

    def add_core(y):
        mine = y_chunk(y)
        s1[mine, :] = (s1[mine, :].astype(F32) + r0[chunk(y), :].astype(F32)).astype(BF16)

    loop(NC // 2, add_core)
    start(NC // 2 - 1, scatter1)

    for copy, sends, takes in backward:
        pl.when(takes)(copy.wait_recv)
        pl.when(sends)(copy.wait_send)

    drightf[0:Q] = dright[...].astype(F32)
    drightf[Q : Q + 16] = dcor[...].astype(F32)
    last = lax.broadcasted_iota(jnp.int32, (16, CM), 0) == 15

    def patch_right(at, value):
        old = dcat[at, Q - 16 : Q, CM : 2 * CM].astype(F32)
        dcat[at, Q - 16 : Q, CM : 2 * CM] = jnp.where(last, value, old).astype(BF16)

    loop(Q, lambda m: patch_right(m, drightf[pl.ds(m, 1), :]))
    patch_right(Q, drightf[Q : Q + 1, :])

    def pass3(b):
        i0 = b * 8
        here = dcat[pl.ds(i0, 8)].reshape(8 * Q, 2 * CM)
        below = dcat[pl.ds(i0 + 1, 8)].reshape(8 * Q, 2 * CM)
        eo[0] = dot_nt(here, wback[0]).reshape(8, Q, 2 * CM)
        eo[1] = (dot_nt(here, wback[1]) + dot_nt(below, wback[2])).reshape(8, Q, 2 * CM)

        def some_rows(c):
            for rp in range(2):
                at = 2 * (i0 + 4 * c)
                for cp in range(2):
                    half, scale = (
                        jnp.concatenate([ref[at + 2 * i + rp, pl.ds(cp, Q, stride=2), :] for i in range(4)], axis=0)
                        for ref in (pre, prs)
                    )
                    g = eo[rp, pl.ds(4 * c, 4), :, lanes(cp)].reshape(4 * Q, CM)
                    d = act_vjp(half, scale, g, ones_m)
                    for i in range(4):
                        natb[rp, i, pl.ds(cp, Q, stride=2), :] = d[i * Q : (i + 1) * Q]
                for i in range(4):
                    prg16[at + 2 * i + rp] = natb[rp, i].astype(BF16)

        unrolled(2, some_rows)
        rows = pl.ds(2 * i0, 16)
        a_wr[...] += dot_tn(prg16[rows].reshape(16 * H, CM), img[rows].reshape(16 * H, CI))

    loop(3, pass3)
    finish(NC // 2 - 1, scatter1)
    r1[cy] = s1[y_chunk(cy), :]
    a1[...] = sum(r1[p].astype(F32) for p in range(NC // 2))
    start(ng - 1, scatter2)
    loop(3, lambda b: pass3(b + 3))

    for p in range(NC):
        s5[p, 32:40, :] = jnp.zeros((8, CM), F32)
        if p < 5:
            s5[p, 32:33, :] = a_misc[p : p + 1, :]
    for half in range(2):
        t = a_wr[:, lanes(half)].T * SCALE
        for p in range(4):
            s5[half * 4 + p, 0:32, :] = t[p * 32 : (p + 1) * 32, :]
    start(NC - 1, scatter5)

    def pass4(k):
        main = dot_nt(prg16[pl.ds(k * 8, 8)].reshape(8 * H, CM), wr[...])
        side = dot_nt(pg[pl.ds(k * 4 * Q, 4 * Q), :], wp[...])
        for m in range(4):
            at = k * 8 + 2 * m
            for half in range(2):
                ob[half, m] = main[2 * m * H : (2 * m + 1) * H, lanes(half)]
                ob[half, m, pl.ds(0, Q, stride=2), :] += side[m * Q : (m + 1) * Q, lanes(half)]
                gimg_hbm[0, at, :, lanes(half)] = ob[half, m].astype(BF16)
            gimg_hbm[0, at + 1] = main[(2 * m + 1) * H : (2 * m + 2) * H].astype(BF16)

    def some(lo, hi):
        loop(hi - lo, lambda k: pass4(lo + k))

    finish(ng - 1, scatter2)
    r2[grp] = a1[piece(grp), :]
    a3[piece(grp), :] = sum(r2[p] for p in range(ng)) * SCALE
    start(ng - 1, gather3)
    some(0, 4)
    finish(NC - 1, scatter5)
    r5[col] = s5[col]
    a5[...] = sum(r5[p] for p in range(NC))
    r6[grp] = a5[...]
    start(ng - 1, gather6)
    some(4, 6)
    finish(ng - 1, gather3)
    s3[...] = a3[...].astype(BF16)
    r4[y_chunk(cy), :] = s3[...]
    start(NC // 2 - 1, gather4)
    some(6, 9)
    finish(ng - 1, gather6)
    a7[...] = sum(r6[p] for p in range(ng))
    r7[col] = a7[...]
    start(NC - 1, gather7)
    some(9, 12)
    finish(NC // 2 - 1, gather4)
    start(1, gather8)
    finish(NC - 1, gather7)
    finish(1, gather8)

    for p in range(3):
        o_spatial[p * CHUNK : (p + 1) * CHUNK, :] = r4[p * CHUNK : (p + 1) * CHUNK, :].astype(F32)

    def summed(at, n):
        return r4[at : at + n, :].astype(F32)

    for q in range(4):
        o_expand[:, q * CM : (q + 1) * CM] = summed(1152 + q * 128, 128)
        for part in range(2):
            o_project[part * 128 : (part + 1) * 128, q * CM : (q + 1) * CM] = summed(1664 + q * 256 + part * 128, 128)
    for p in range(NC):
        o_reduce[p * 32 : (p + 1) * 32, :] = r7[p, 0:32, :]
    for k in range(4):
        o_classify[0:1, lanes(k)] = -r7[k, 32:33, :]
        o_classify[1:2, lanes(k)] = r7[k, 32:33, :]
    o_loss[...] = r7[4, 32:33, 0:1]


def hand_over(*refs):
    n = (len(refs) - 1) // 2
    given, taken, sem = refs[:n], refs[n : 2 * n], refs[-1]
    copies = [pltpu.make_async_copy(a, b, sem.at[k]) for k, (a, b) in enumerate(zip(given, taken))]
    for c in copies:
        c.start()
    for c in copies:
        c.wait()


def per_device(image, wr, ws, we, wp, wc, mask, label):
    vmem = pl.BlockSpec(memory_space=pltpu.VMEM)
    hbm = pl.BlockSpec(memory_space=pl.ANY)
    v = pltpu.VMEM
    dma = pltpu.SemaphoreType.DMA
    scratch = [
        v((CI, CM), BF16),
        v((3, 3 * CM, CM), BF16),
        v((CM, CO), BF16),
        v((CI, CO), BF16),
        v((H, H, CI), BF16),
        v((H, H, CM), F32),
        v((H, H, CM), F32),
        v((8, 8 + H, CM), F32),
        v((Q + 1, Q, 3 * CM), BF16),
        v((Q, Q, 3 * CM), BF16),
        v((Q, Q, CI), BF16),
        v((2, H, CM), F32),
        v((H, CM), F32),
        v((H, CM), BF16),
        v((H, CM), BF16),
        v((16, CM), BF16),
        v((H + 16, CM), F32),
        v((Q, 3 * CM), BF16),
        v((2, TB * Q, CM), F32),
        v((TB * Q, CM), BF16),
        v((TB * Q, CO), F32),
        v((Q * Q, CO), F32),
        v((TB * Q, CM), F32),
        v((Q * Q, CM), F32),
        v((Q, CO), F32),
        v((Q, CO), F32),
        v((4 * Q, CO), F32),
        v((TB * Q, CO), BF16),
        v((Q * Q, CO), BF16),
        v((8, Q + 8, CM), F32),
        v((Q + 1, Q, 2 * CM), BF16),
        v((3, 2 * CM, 2 * CM), BF16),
        v((2, 8, Q, 2 * CM), F32),
        v((2, 4, H, CM), F32),
        v((H, H, CM), BF16),
        v((Q, CM), BF16),
        v((16, CM), BF16),
        v((Q + 16, CM), F32),
        v((Q, 2 * CM), BF16),
        v((Q, CM), F32),
        v((2, 4, H, CM), F32),
        v((CM, 9 * CM), F32),
        v((CM, CO), F32),
        v((CI, CO), F32),
        v((CM, CI), F32),
        v((8, CM), F32),
        v((NC * CHUNK, CM), BF16),
        v((NC // 2 * CHUNK, CM), BF16),
        v((NC // 2, CHUNK, CM), BF16),
        v((CHUNK, CM), F32),
        v((NR * NS, PIECE, CM), F32),
        v((CHUNK, CM), F32),
        v((CHUNK, CM), BF16),
        v((NC * CHUNK, CM), BF16),
        v((NC, 40, CM), F32),
        v((NC, 40, CM), F32),
        v((40, CM), F32),
        v((NR * NS, 40, CM), F32),
        v((40, CM), F32),
        v((NC, 40, CM), F32),
        dma((IMG_CHUNKS,)),
        dma((4,)),
        dma((6,)),
        dma((6,)),
        dma((2,)),
        dma((2, NC)),
        dma((2, NR * NS)),
        dma((2, NR * NS)),
        dma((2, NC)),
        dma((2, NC)),
        dma((2, NR * NS)),
        dma((2, NC)),
        dma((2,)),
    ]
    shapes = [image.shape, (CI, CM), (9 * CM, CM), (CM, CO), (CI, CO), (2, CO), (1, 1)]
    out = pl.pallas_call(
        kernel,
        out_shape=[v(s, BF16 if k == 0 else F32) for k, s in enumerate(shapes)],
        in_specs=[hbm] * 5 + [vmem] * 2 + [pl.BlockSpec(memory_space=pltpu.SMEM)],
        out_specs=[vmem] * 7,
        scratch_shapes=scratch,
        compiler_params=pltpu.CompilerParams(
            collective_id=0, has_side_effects=True, vmem_limit_bytes=50 * 1024 * 1024
        ),
        cost_estimate=pl.CostEstimate(flops=7_000_000_000, bytes_accessed=12_000_000, transcendentals=4_000_000),
    )(image, wr, ws.reshape(3, 3 * CM, CM), we, wp, wc.T, jnp.transpose(mask, (1, 0, 2)), label)
    out = pl.pallas_call(
        hand_over,
        out_shape=[jax.ShapeDtypeStruct(o.shape, o.dtype) for o in out],
        in_specs=[vmem] * len(out),
        out_specs=[hbm] * len(out),
        scratch_shapes=[dma((len(out),))],
        compiler_params=pltpu.CompilerParams(vmem_limit_bytes=1024 * 1024),
    )(*out)
    grad_image, g_reduce, g_spatial, g_expand, g_project, g_classify, loss = out
    return grad_image, g_reduce, g_spatial.reshape(3, 3, CM, CM), g_expand, g_project, g_classify.T, loss[0, 0]


def solution(mesh):
    in_specs = (P("slide", "row", "col", None), P(), P(), P(), P(), P(), P("slide", None, None), P("slide"))
    out_specs = (P("slide", "row", "col", None), P(), P(), P(), P(), P(), P())
    return jax.shard_map(per_device, mesh=mesh, in_specs=in_specs, out_specs=out_specs, check_vma=False)
```

```python
import jax
import jax.numpy as jnp
from jax import lax
from jax.experimental import pallas as pl
from jax.experimental.pallas import tpu as pltpu
from jax.sharding import PartitionSpec as P

EPSILON = 1e-05
MESH = pl.DeviceIdType.MESH
F32 = jnp.float32
BF16 = jnp.bfloat16

NR, NC, NS = 4, 8, 4
H = 96
Q = 48
CI, CM, CO = 256, 128, 512
TB = 16
SCALE = 1.0 / 288.0
CHUNK = 384
PIECE = CHUNK // (NR * NS)
IMG_CHUNKS = 12


def dot(a, b):
    return lax.dot_general(a, b, (((1,), (0,)), ((), ())), preferred_element_type=F32)


def dot_nt(a, b):
    return lax.dot_general(a, b, (((1,), (1,)), ((), ())), preferred_element_type=F32)


def dot_tn(a, b):
    return lax.dot_general(a, b, (((0,), (0,)), ((), ())), preferred_element_type=F32)


def lane_mean(x, ones):
    return dot(x.astype(BF16), ones)


def half_scale(squares, ones):
    return lax.rsqrt(lane_mean(squares, ones) + 4.0 * EPSILON)


def silu_vjp(half, g):
    t = jnp.tanh(half)
    return g * (1.0 + t) * (1.0 + half * (1.0 - t))


def silu(half):
    return half * jnp.tanh(half) + half


def act_vjp(half, scale, g, ones):
    dn = silu_vjp(half, g)
    return scale * (dn - half * lane_mean(dn * half, ones))


def lanes(k):
    return slice(k * CM, (k + 1) * CM)


def loop(n, body):
    def step(i, carry):
        body(i)
        return carry

    lax.fori_loop(0, n, step, 0)


def unrolled(n, body):
    for i in range(n):
        body(i)


def kernel(
    img_hbm, wr_hbm, ws_hbm, we_hbm, wp_hbm, wc, mask, label,
    gimg_hbm, o_reduce, o_spatial, o_expand, o_project, o_classify, o_loss,
    wr, ws, we, wp, img, pre, prs, actb, rc_odd, rc_even, evp, evb, colb, col16, hcol, hcor, hcolf, srow,
    psp, spat, ne, npj, r_e, r_p, feat, gb, dnb, eg, pg, dbuf, dcat, wback, eo, natb, prg16,
    dright, dcor, drightf, drow, dcol, ob,
    a_ws, a_we, a_wp, a_wr, a_misc,
    s1, r0, r1, a1, r2, a3, s3, r4, s5, r5, a5, r6, a7, r7,
    sem_in, sem_w, sem_h, sem_g, sem0, sem1, sem2, sem3, sem4, sem5, sem6, sem7, sem8,
):
    row, col, sld = lax.axis_index("row"), lax.axis_index("col"), lax.axis_index("slide")
    grp = row * NS + sld
    has_up, has_down = row > 0, row < NR - 1
    has_left, has_right = col > 0, col < NC - 1

    rows_in = H // IMG_CHUNKS

    def image_copy(k):
        return pltpu.make_async_copy(
            img_hbm.at[0, pl.ds(k * rows_in, rows_in)], img.at[pl.ds(k * rows_in, rows_in)], sem_in.at[k]
        )

    weights = [
        pltpu.make_async_copy(a, b, sem_w.at[k])
        for k, (a, b) in enumerate(((wr_hbm, wr), (ws_hbm, ws), (we_hbm, we), (wp_hbm, wp)))
    ]
    weights[0].start()
    loop(IMG_CHUNKS, lambda k: image_copy(k).start())
    for copy in weights[1:]:
        copy.start()

    def col_peer(d):
        return {"col": lax.rem(col + d, NC)}

    def grp_peer(d):
        q = lax.rem(grp + d, NR * NS)
        return {"row": q // NS, "slide": lax.rem(q, NS)}

    barrier = pltpu.get_barrier_semaphore()
    loop(NC - 1, lambda d: pl.semaphore_signal(barrier, inc=1, device_id=col_peer(d + 1), device_id_type=MESH))
    loop(NR * NS - 1, lambda d: pl.semaphore_signal(barrier, inc=1, device_id=grp_peer(d + 1), device_id_type=MESH))
    to_diag = has_down & has_right
    from_diag = has_up & has_left

    @pl.when(to_diag)
    def _():
        pl.semaphore_signal(barrier, inc=1, device_id={"row": row + 1, "col": col + 1}, device_id_type=MESH)

    @pl.when(from_diag)
    def _():
        pl.semaphore_signal(barrier, inc=1, device_id={"row": row - 1, "col": col - 1}, device_id_type=MESH)

    actb[:, 0:8, :] = jnp.zeros_like(actb[:, 0:8, :])
    dbuf[:, Q : Q + 8, :] = jnp.zeros_like(dbuf[:, Q : Q + 8, :])
    ones_m = jnp.full((CM, CM), 4.0 / CM, BF16)
    ones_o = jnp.full((CM, CM), 4.0 / CO, BF16)

    @pl.when(jnp.logical_not(has_up))
    def _():
        rc_odd[0] = jnp.zeros_like(rc_odd[0])

    @pl.when(jnp.logical_not(has_left))
    def _():
        hcol[...] = jnp.zeros_like(hcol)

    @pl.when(jnp.logical_not(from_diag))
    def _():
        hcor[...] = jnp.zeros_like(hcor)

    @pl.when(jnp.logical_not(has_down))
    def _():
        dcat[Q] = jnp.zeros_like(dcat[Q])

    @pl.when(jnp.logical_not(has_right))
    def _():
        dright[...] = jnp.zeros_like(dright)

    @pl.when(jnp.logical_not(to_diag))
    def _():
        dcor[...] = jnp.zeros_like(dcor)

    drow_w = wc[1:2, :] - wc[0:1, :]
    sign = 1.0 - 2.0 * label[0].astype(F32)
    tissue_all = mask[...].astype(F32)
    tiles = jnp.sum(jnp.sum(tissue_all, axis=0), axis=1, keepdims=True)
    mask_r = lax.broadcasted_iota(jnp.int32, mask.shape, 0)
    mask_c = lax.broadcasted_iota(jnp.int32, mask.shape, 2)

    weights[0].wait()

    def pass1(k):
        image_copy(k).wait()
        x = img[pl.ds(k * 8, 8)].reshape(8 * H, CI)
        v = dot(x, wr[...])
        scale = half_scale(v * v, ones_m)
        half = v * scale
        pre[pl.ds(k * 8, 8)] = half.reshape(8, H, CM)
        prs[pl.ds(k * 8, 8)] = scale.reshape(8, H, CM)
        actb[:, 8 : 8 + H, :] = silu(half).reshape(8, H, CM)
        for r in range(8):
            rows, at = (rc_even, k * 4 + r // 2) if r % 2 == 0 else (rc_odd, k * 4 + r // 2 + 1)
            for b in range(3):
                rows[at, :, b * CM : (b + 1) * CM] = actb[r, pl.ds(7 + b, Q, stride=2), :].astype(BF16)
            colb[pl.ds(k * 8 + r, 1), :] = actb[r, 7 + H : 8 + H, :]

    loop(IMG_CHUNKS, pass1)

    col16[...] = colb[...].astype(BF16)
    srow[...] = rc_odd[Q]

    def remote(src, dst, send, recv, device):
        return pltpu.make_async_remote_copy(
            src_ref=src, dst_ref=dst, send_sem=send, recv_sem=recv, device_id=device, device_id_type=MESH
        )

    down = remote(srow, rc_odd.at[0], sem_h.at[0], sem_h.at[1], {"row": lax.rem(row + 1, NR)})
    right = remote(col16, hcol, sem_h.at[2], sem_h.at[3], {"col": lax.rem(col + 1, NC)})
    diag = remote(
        col16.at[pl.ds(H - 16, 16)], hcor, sem_h.at[4], sem_h.at[5],
        {"row": lax.rem(row + 1, NR), "col": lax.rem(col + 1, NC)},
    )
    n_diag = jnp.where(to_diag, 1, 0) + jnp.where(from_diag, 1, 0)
    pl.semaphore_wait(barrier, NC - 1 + NR * NS - 1 + n_diag)
    forward = ((down, has_down, has_up), (right, has_right, has_left), (diag, to_diag, from_diag))
    for copy, sends, _ in forward:
        pl.when(sends)(copy.start)

    a_ws[...] = jnp.zeros_like(a_ws)
    a_we[...] = jnp.zeros_like(a_we)
    a_wp[...] = jnp.zeros_like(a_wp)
    a_wr[...] = jnp.zeros_like(a_wr)
    a_misc[...] = jnp.zeros_like(a_misc)
    for copy in weights[1:]:
        copy.wait()
    wback[...] = jnp.zeros_like(wback)

    def tap(a, b):
        return ws[a, b * CM : (b + 1) * CM, :]

    for slot, a in ((0, 1), (1, 2), (2, 0)):
        wback[slot, 0:CM, 0:CM] = tap(a, 1)
        wback[slot, CM : 2 * CM, 0:CM] = tap(a, 2)
        wback[slot, CM : 2 * CM, CM : 2 * CM] = tap(a, 0)
    def even_rows(m):
        x = img[2 * m].astype(F32)
        for half in range(2):
            evb[half] = x[:, half * CM : (half + 1) * CM]
        for half in range(2):
            evp[m, :, half * CM : (half + 1) * CM] = evb[half, pl.ds(0, Q, stride=2), :].astype(BF16)

    loop(Q // 4, lambda m: unrolled(4, lambda i: even_rows(4 * m + i)))

    def project(b):
        at = pl.ds(b * 8 * Q, 8 * Q)
        p = dot(evp[pl.ds(b * 8, 8)].reshape(8 * Q, CI), wp[...])
        npj[at, :] = p
        r_p[at, :] = half_scale(sum(p[:, lanes(k)] * p[:, lanes(k)] for k in range(4)), ones_o)

    loop(3, lambda b: unrolled(2, lambda i: project(2 * b + i)))

    for copy, sends, takes in forward:
        pl.when(takes)(copy.wait_recv)
        pl.when(sends)(copy.wait_send)

    hcolf[0:H] = hcol[...].astype(F32)
    hcolf[H : H + 16] = hcor[...].astype(F32)
    first = lax.broadcasted_iota(jnp.int32, (16, CM), 0) == 0

    def patch_left(rows, at, value):
        old = rows[at, 0:16, 0:CM].astype(F32)
        rows[at, 0:16, 0:CM] = jnp.where(first, value, old).astype(BF16)

    patch_left(rc_odd, 0, hcolf[H + 15 : H + 16, :])

    def patch_rows(m):
        patch_left(rc_even, m, hcolf[pl.ds(2 * m, 1), :])
        patch_left(rc_odd, m + 1, hcolf[pl.ds(2 * m + 1, 1), :])

    loop(Q // 4, lambda m: unrolled(4, lambda i: patch_rows(4 * m + i)))

    ng = NR * NS

    def start(n, make):
        loop(n, lambda d: make(d + 1).start())

    def finish(n, make):
        loop(n, lambda d: make(d + 1).wait())

    def chunk(p):
        return pl.ds(pl.multiple_of(p * CHUNK, CHUNK), CHUNK)

    def piece(p):
        return pl.ds(pl.multiple_of(p * PIECE, PIECE), PIECE)

    core, cy = lax.rem(col, 2), col // 2
    half_rows = NC // 2 * CHUNK

    def y_chunk(y):
        return chunk(core * (NC // 2) + y)

    other = {"col": col + 1 - 2 * core}

    def scatter0(part):
        size = half_rows // 2
        src = s1.at[pl.ds(pl.multiple_of((1 - core) * half_rows + part * size, size), size)]
        return remote(src, r0.at[pl.ds(part * size, size)], sem0.at[0, part], sem0.at[1, part], other)

    def add_part(part):
        scatter0(part).wait()
        for y in (2 * part, 2 * part + 1):
            mine = y_chunk(y)
            s1[mine, :] = (s1[mine, :].astype(F32) + r0[y * CHUNK : (y + 1) * CHUNK, :].astype(F32)).astype(BF16)
        for d in range(1, NC // 2):
            pl.when(lax.rem(cy + d, NC // 2) // 2 == part)(scatter1(d).start)

    def scatter1(d):
        peer = lax.rem(cy + d, NC // 2)
        return remote(s1.at[y_chunk(peer)], r1.at[cy], sem1.at[0, d], sem1.at[1, d], {"col": 2 * peer + core})

    def scatter2(d):
        q = lax.rem(grp + d, ng)
        return remote(a1.at[piece(q)], r2.at[grp], sem2.at[0, d], sem2.at[1, d], grp_peer(d))

    def gather3(d):
        return remote(a3.at[piece(grp)], a3.at[piece(grp)], sem3.at[0, d], sem3.at[1, d], grp_peer(d))

    def gather4(d):
        peer = lax.rem(cy + d, NC // 2)
        return remote(s3, r4.at[y_chunk(cy)], sem4.at[0, d], sem4.at[1, d], {"col": 2 * peer + core})

    def gather8(d):
        there = r4.at[y_chunk(lax.rem(cy - d + NC // 2, NC // 2))]
        return remote(there, there, sem8.at[0, d], sem8.at[1, d], other)

    def scatter5(d):
        peer = lax.rem(col + d, NC)
        return remote(s5.at[peer], r5.at[col], sem5.at[0, d], sem5.at[1, d], {"col": peer})

    def gather6(d):
        return remote(a5, r6.at[grp], sem6.at[0, d], sem6.at[1, d], grp_peer(d))

    def gather7(d):
        return remote(a7, r7.at[col], sem7.at[0, d], sem7.at[1, d], col_peer(d))

    npx = TB * Q

    def taps(a, at, n):
        if a == 1:
            return rc_even[pl.ds(at, n)].reshape(n * Q, 3 * CM)
        return rc_odd[pl.ds(at + a // 2, n)].reshape(n * Q, 3 * CM)

    def spatial_weight_grad(u):
        d16 = dcat[pl.ds(u * TB, TB), :, 0:CM].reshape(npx, CM)
        for a in range(3):
            a_ws[:, a * 3 * CM : (a + 1) * 3 * CM] += dot_tn(d16, taps(a, u * TB, TB))

    def tile_row(u):
        i0 = u * TB

        def convolve(b):
            at = i0 + b * 8
            v = sum(dot(taps(a, at, 8), ws[a]) for a in range(3))
            scale = half_scale(v * v, ones_m)
            half = v * scale
            psp[0, pl.ds(b * 8 * Q, 8 * Q), :] = half
            psp[1, pl.ds(b * 8 * Q, 8 * Q), :] = scale
            spat[pl.ds(b * 8 * Q, 8 * Q), :] = silu(half).astype(BF16)

        unrolled(2, convolve)

        def expand(b):
            at = pl.ds(b * 8 * Q, 8 * Q)
            e = dot(spat[at, :], we[...])
            ne[at, :] = e
            r_e[at, :] = half_scale(sum(e[:, lanes(k)] * e[:, lanes(k)] for k in range(4)), ones_o)

        unrolled(2, expand)
        feat[...] = jnp.zeros_like(feat)

        def merge(b):
            at = pl.ds(b * 4 * Q, 4 * Q)
            out = pl.ds(i0 * Q + b * 4 * Q, 4 * Q)
            h_e, h_p = r_e[at, :], r_p[out, :]
            for k in range(4):
                half = ne[at, lanes(k)] * h_e + npj[out, lanes(k)] * h_p
                feat[:, lanes(k)] += jnp.sum(silu(half).reshape(4, Q, CM), axis=0)

        loop(4, merge)

        for v in range(3):
            f = jnp.sum(feat[v * TB : (v + 1) * TB, :], axis=0, keepdims=True) * (1.0 / (TB * TB))
            margin = jnp.sum(f * drow_w, axis=1, keepdims=True) * sign
            here = (mask_r == row * 3 + u) & (mask_c == col * 3 + v)
            tissue = jnp.where(here, tissue_all, 0.0)
            tissue = jnp.sum(jnp.sum(tissue, axis=0), axis=1, keepdims=True)
            soft = jnp.maximum(margin, 0.0) + jnp.log(1.0 + jnp.exp(-jnp.abs(margin)))
            weight = tissue * (0.5 + 0.5 * jnp.tanh(0.5 * margin)) / tiles * sign
            for k in range(CO // CM):
                a_misc[k : k + 1, :] += f[:, k * CM : (k + 1) * CM] * weight
            a_misc[4:5, :] += jnp.broadcast_to(tissue * soft / tiles, (1, CM))
            gb[v * TB : (v + 1) * TB, :] = jnp.broadcast_to(drow_w * (weight * 288.0), (TB, CO))

        def unmerge(b):
            at = pl.ds(b * 4 * Q, 4 * Q)
            out = pl.ds(i0 * Q + b * 4 * Q, 4 * Q)
            s_e, s_p = r_e[at, :], r_p[out, :]
            z_e, z_p = 0.0, 0.0
            for k in range(4):
                n_e, n_p = ne[at, lanes(k)] * s_e, npj[out, lanes(k)] * s_p
                dn = silu_vjp((n_e + n_p).reshape(4, Q, CM), gb[:, lanes(k)][None]).reshape(4 * Q, CM)
                dnb[:, lanes(k)] = dn
                z_e, z_p = z_e + dn * n_e, z_p + dn * n_p
            m_e, m_p = lane_mean(z_e, ones_o), lane_mean(z_p, ones_o)
            for k in range(4):
                dn = dnb[:, lanes(k)]
                n_e, n_p = ne[at, lanes(k)] * s_e, npj[out, lanes(k)] * s_p
                eg[at, lanes(k)] = (s_e * (dn - n_e * m_e)).astype(BF16)
                pg[out, lanes(k)] = (s_p * (dn - n_p * m_p)).astype(BF16)

        loop(4, unmerge)

        a_we[...] += dot_tn(spat[...], eg[...])
        a_wp[...] += dot_tn(evp[pl.ds(i0, TB)].reshape(npx, CI), pg[pl.ds(i0 * Q, npx), :])

    def back_row(u):
        i0 = u * TB

        def unconvolve(b):
            at = pl.ds(b * 8 * Q, 8 * Q)
            g = dot_nt(eg[at, :], we[...])
            d = act_vjp(psp[0, at, :], psp[1, at, :], g, ones_m)
            dbuf[:, 0:Q, :] = d.reshape(8, Q, CM)
            d16 = d.astype(BF16)
            dcat[pl.ds(i0 + b * 8, 8), :, 0:CM] = d16.reshape(8, Q, CM)
            for r in range(8):
                dcat[i0 + b * 8 + r, :, CM : 2 * CM] = dbuf[r, 1 : Q + 1, :].astype(BF16)
                dcol[pl.ds(i0 + b * 8 + r, 1), :] = dbuf[r, 0:1, :]

        unrolled(2, unconvolve)

    def both(u):
        tile_row(u)
        back_row(u)
        spatial_weight_grad(u)

    e_slot, s_slot = (0, 1, 4, 5), (2, 3, 6)

    def e_rows(r):
        at = e_slot[r // CHUNK] * CHUNK + r % CHUNK
        return slice(at, at + CM)

    def s_rows(t):
        at = s_slot[t // 3] * CHUNK + t % 3 * CM
        return slice(at, at + CM)

    loop(2, both)
    tile_row(2)
    for q in range(4):
        s1[e_rows(q * CM), :] = a_we[:, lanes(q)].astype(BF16)
        for part in range(2):
            s1[e_rows(512 + (2 * q + part) * CM), :] = a_wp[part * CM : (part + 1) * CM, lanes(q)].astype(BF16)
    s1[7 * CHUNK :, :] = jnp.zeros((CHUNK, CM), BF16)
    scatter0(0).start()
    back_row(2)

    drow[...] = dcat[0]
    col16[0:Q] = dcol[...].astype(BF16)
    up = remote(drow, dcat.at[Q], sem_g.at[0], sem_g.at[1], {"row": lax.rem(row + NR - 1, NR)})
    left = remote(col16.at[pl.ds(0, Q)], dright, sem_g.at[2], sem_g.at[3], {"col": lax.rem(col + NC - 1, NC)})
    gaid = remote(
        col16.at[pl.ds(0, 16)], dcor, sem_g.at[4], sem_g.at[5],
        {"row": lax.rem(row + NR - 1, NR), "col": lax.rem(col + NC - 1, NC)},
    )
    backward = ((up, has_up, has_down), (left, has_left, has_right), (gaid, from_diag, to_diag))
    for copy, sends, _ in backward:
        pl.when(sends)(copy.start)

    add_part(0)
    spatial_weight_grad(2)
    for t in range(9):
        s1[s_rows(t), :] = a_ws[:, lanes(t)].T.astype(BF16)
    scatter0(1).start()
    add_part(1)
    for copy, sends, takes in backward:
        pl.when(takes)(copy.wait_recv)
        pl.when(sends)(copy.wait_send)

    drightf[0:Q] = dright[...].astype(F32)
    drightf[Q : Q + 16] = dcor[...].astype(F32)
    last = lax.broadcasted_iota(jnp.int32, (16, CM), 0) == 15

    def patch_right(at, value):
        old = dcat[at, Q - 16 : Q, CM : 2 * CM].astype(F32)
        dcat[at, Q - 16 : Q, CM : 2 * CM] = jnp.where(last, value, old).astype(BF16)

    loop(Q, lambda m: patch_right(m, drightf[pl.ds(m, 1), :]))
    patch_right(Q, drightf[Q : Q + 1, :])

    def pass3(b):
        i0 = b * 8
        here = dcat[pl.ds(i0, 8)].reshape(8 * Q, 2 * CM)
        below = dcat[pl.ds(i0 + 1, 8)].reshape(8 * Q, 2 * CM)
        eo[0] = dot_nt(here, wback[0]).reshape(8, Q, 2 * CM)
        eo[1] = (dot_nt(here, wback[1]) + dot_nt(below, wback[2])).reshape(8, Q, 2 * CM)

        def some_rows(c):
            for rp in range(2):
                at = 2 * (i0 + 4 * c)
                for cp in range(2):
                    half, scale = (
                        jnp.concatenate([ref[at + 2 * i + rp, pl.ds(cp, Q, stride=2), :] for i in range(4)], axis=0)
                        for ref in (pre, prs)
                    )
                    g = eo[rp, pl.ds(4 * c, 4), :, lanes(cp)].reshape(4 * Q, CM)
                    d = act_vjp(half, scale, g, ones_m)
                    for i in range(4):
                        natb[rp, i, pl.ds(cp, Q, stride=2), :] = d[i * Q : (i + 1) * Q]
                for i in range(4):
                    prg16[at + 2 * i + rp] = natb[rp, i].astype(BF16)

        unrolled(2, some_rows)
        rows = pl.ds(2 * i0, 16)
        a_wr[...] += dot_tn(prg16[rows].reshape(16 * H, CM), img[rows].reshape(16 * H, CI))

    loop(3, pass3)
    finish(NC // 2 - 1, scatter1)
    r1[cy] = s1[y_chunk(cy), :]
    a1[...] = sum(r1[p].astype(F32) for p in range(NC // 2))
    start(ng - 1, scatter2)
    loop(3, lambda b: pass3(b + 3))

    for p in range(NC):
        s5[p, 32:40, :] = jnp.zeros((8, CM), F32)
        if p < 5:
            s5[p, 32:33, :] = a_misc[p : p + 1, :]
    for half in range(2):
        t = a_wr[:, lanes(half)].T * SCALE
        for p in range(4):
            s5[half * 4 + p, 0:32, :] = t[p * 32 : (p + 1) * 32, :]
    start(NC - 1, scatter5)

    def pass4(k):
        main = dot_nt(prg16[pl.ds(k * 8, 8)].reshape(8 * H, CM), wr[...])
        side = dot_nt(pg[pl.ds(k * 4 * Q, 4 * Q), :], wp[...])
        for m in range(4):
            at = k * 8 + 2 * m
            for half in range(2):
                ob[half, m] = main[2 * m * H : (2 * m + 1) * H, lanes(half)]
                ob[half, m, pl.ds(0, Q, stride=2), :] += side[m * Q : (m + 1) * Q, lanes(half)]
                gimg_hbm[0, at, :, lanes(half)] = ob[half, m].astype(BF16)
            gimg_hbm[0, at + 1] = main[(2 * m + 1) * H : (2 * m + 2) * H].astype(BF16)

    def some(lo, hi):
        loop(hi - lo, lambda k: pass4(lo + k))

    finish(ng - 1, scatter2)
    r2[grp] = a1[piece(grp), :]
    a3[piece(grp), :] = sum(r2[p] for p in range(ng)) * SCALE
    start(ng - 1, gather3)
    some(0, 4)
    finish(NC - 1, scatter5)
    r5[col] = s5[col]
    a5[...] = sum(r5[p] for p in range(NC))
    r6[grp] = a5[...]
    start(ng - 1, gather6)
    some(4, 6)
    finish(ng - 1, gather3)
    s3[...] = a3[...].astype(BF16)
    r4[y_chunk(cy), :] = s3[...]
    start(NC // 2 - 1, gather4)
    gather8(0).start()
    some(6, 9)
    finish(ng - 1, gather6)
    a7[...] = sum(r6[p] for p in range(ng))
    r7[col] = a7[...]
    start(NC - 1, gather7)
    some(9, 12)
    for d in range(1, NC // 2):
        gather4(d).wait_recv()
        gather8(d).start()
    finish(NC - 1, gather7)
    for d in range(1, NC // 2):
        gather4(d).wait_send()
    for d in range(NC // 2):
        gather8(d).wait()

    for t in range(9):
        o_spatial[t * CM : (t + 1) * CM, :] = r4[s_rows(t), :].astype(F32)
    for q in range(4):
        o_expand[:, lanes(q)] = r4[e_rows(q * CM), :].astype(F32)
        for part in range(2):
            o_project[part * CM : (part + 1) * CM, lanes(q)] = r4[e_rows(512 + (2 * q + part) * CM), :].astype(F32)
    for p in range(NC):
        o_reduce[p * 32 : (p + 1) * 32, :] = r7[p, 0:32, :]
    for k in range(4):
        o_classify[0:1, lanes(k)] = -r7[k, 32:33, :]
        o_classify[1:2, lanes(k)] = r7[k, 32:33, :]
    o_loss[...] = r7[4, 32:33, 0:1]


def hand_over(*refs):
    n = (len(refs) - 1) // 2
    given, taken, sem = refs[:n], refs[n : 2 * n], refs[-1]
    copies = [pltpu.make_async_copy(a, b, sem.at[k]) for k, (a, b) in enumerate(zip(given, taken))]
    for c in copies:
        c.start()
    for c in copies:
        c.wait()


def per_device(image, wr, ws, we, wp, wc, mask, label):
    vmem = pl.BlockSpec(memory_space=pltpu.VMEM)
    hbm = pl.BlockSpec(memory_space=pl.ANY)
    v = pltpu.VMEM
    dma = pltpu.SemaphoreType.DMA
    scratch = [
        v((CI, CM), BF16),
        v((3, 3 * CM, CM), BF16),
        v((CM, CO), BF16),
        v((CI, CO), BF16),
        v((H, H, CI), BF16),
        v((H, H, CM), F32),
        v((H, H, CM), F32),
        v((8, 8 + H, CM), F32),
        v((Q + 1, Q, 3 * CM), BF16),
        v((Q, Q, 3 * CM), BF16),
        v((Q, Q, CI), BF16),
        v((2, H, CM), F32),
        v((H, CM), F32),
        v((H, CM), BF16),
        v((H, CM), BF16),
        v((16, CM), BF16),
        v((H + 16, CM), F32),
        v((Q, 3 * CM), BF16),
        v((2, TB * Q, CM), F32),
        v((TB * Q, CM), BF16),
        v((TB * Q, CO), F32),
        v((Q * Q, CO), F32),
        v((TB * Q, CM), F32),
        v((Q * Q, CM), F32),
        v((Q, CO), F32),
        v((Q, CO), F32),
        v((4 * Q, CO), F32),
        v((TB * Q, CO), BF16),
        v((Q * Q, CO), BF16),
        v((8, Q + 8, CM), F32),
        v((Q + 1, Q, 2 * CM), BF16),
        v((3, 2 * CM, 2 * CM), BF16),
        v((2, 8, Q, 2 * CM), F32),
        v((2, 4, H, CM), F32),
        v((H, H, CM), BF16),
        v((Q, CM), BF16),
        v((16, CM), BF16),
        v((Q + 16, CM), F32),
        v((Q, 2 * CM), BF16),
        v((Q, CM), F32),
        v((2, 4, H, CM), F32),
        v((CM, 9 * CM), F32),
        v((CM, CO), F32),
        v((CI, CO), F32),
        v((CM, CI), F32),
        v((8, CM), F32),
        v((NC * CHUNK, CM), BF16),
        v((NC // 2 * CHUNK, CM), BF16),
        v((NC // 2, CHUNK, CM), BF16),
        v((CHUNK, CM), F32),
        v((NR * NS, PIECE, CM), F32),
        v((CHUNK, CM), F32),
        v((CHUNK, CM), BF16),
        v((NC * CHUNK, CM), BF16),
        v((NC, 40, CM), F32),
        v((NC, 40, CM), F32),
        v((40, CM), F32),
        v((NR * NS, 40, CM), F32),
        v((40, CM), F32),
        v((NC, 40, CM), F32),
        dma((IMG_CHUNKS,)),
        dma((4,)),
        dma((6,)),
        dma((6,)),
        dma((2, 2)),
        dma((2, NC)),
        dma((2, NR * NS)),
        dma((2, NR * NS)),
        dma((2, NC)),
        dma((2, NC)),
        dma((2, NR * NS)),
        dma((2, NC)),
        dma((2, NC)),
    ]
    shapes = [image.shape, (CI, CM), (9 * CM, CM), (CM, CO), (CI, CO), (2, CO), (1, 1)]
    out = pl.pallas_call(
        kernel,
        out_shape=[v(s, BF16 if k == 0 else F32) for k, s in enumerate(shapes)],
        in_specs=[hbm] * 5 + [vmem] * 2 + [pl.BlockSpec(memory_space=pltpu.SMEM)],
        out_specs=[vmem] * 7,
        scratch_shapes=scratch,
        compiler_params=pltpu.CompilerParams(
            collective_id=0, has_side_effects=True, vmem_limit_bytes=50 * 1024 * 1024
        ),
        cost_estimate=pl.CostEstimate(flops=7_000_000_000, bytes_accessed=12_000_000, transcendentals=4_000_000),
    )(image, wr, ws.reshape(3, 3 * CM, CM), we, wp, wc.T, jnp.transpose(mask, (1, 0, 2)), label)
    out = pl.pallas_call(
        hand_over,
        out_shape=[jax.ShapeDtypeStruct(o.shape, o.dtype) for o in out],
        in_specs=[vmem] * len(out),
        out_specs=[hbm] * len(out),
        scratch_shapes=[dma((len(out),))],
        compiler_params=pltpu.CompilerParams(vmem_limit_bytes=1024 * 1024),
    )(*out)
    grad_image, g_reduce, g_spatial, g_expand, g_project, g_classify, loss = out
    return grad_image, g_reduce, g_spatial.reshape(3, 3, CM, CM), g_expand, g_project, g_classify.T, loss[0, 0]


def solution(mesh):
    in_specs = (P("slide", "row", "col", None), P(), P(), P(), P(), P(), P("slide", None, None), P("slide"))
    out_specs = (P("slide", "row", "col", None), P(), P(), P(), P(), P(), P())
    return jax.shard_map(per_device, mesh=mesh, in_specs=in_specs, out_specs=out_specs, check_vma=False)
```

```python
import jax
import jax.numpy as jnp
from jax import lax
from jax.experimental import pallas as pl
from jax.experimental.pallas import tpu as pltpu
from jax.sharding import PartitionSpec as P

EPSILON = 1e-05
MESH = pl.DeviceIdType.MESH
F32 = jnp.float32
BF16 = jnp.bfloat16

NR, NC, NS = 4, 8, 4
H = 96
Q = 48
CI, CM, CO = 256, 128, 512
TB = 16
SCALE = 1.0 / 288.0
CHUNK = 384
PIECE = CHUNK // (NR * NS)
IMG_CHUNKS = 12


def dot(a, b):
    return lax.dot_general(a, b, (((1,), (0,)), ((), ())), preferred_element_type=F32)


def dot_nt(a, b):
    return lax.dot_general(a, b, (((1,), (1,)), ((), ())), preferred_element_type=F32)


def dot_tn(a, b):
    return lax.dot_general(a, b, (((0,), (0,)), ((), ())), preferred_element_type=F32)


def lane_mean(x, ones):
    return dot(x.astype(BF16), ones)


def half_scale(squares, ones):
    return lax.rsqrt(lane_mean(squares, ones) + 4.0 * EPSILON)


def silu_vjp(half, g):
    t = jnp.tanh(half)
    return g * (1.0 + t) * (1.0 + half * (1.0 - t))


def silu(half):
    return half * jnp.tanh(half) + half


def act_vjp(half, scale, g, ones):
    dn = silu_vjp(half, g)
    return scale * (dn - half * lane_mean(dn * half, ones))


def lanes(k):
    return slice(k * CM, (k + 1) * CM)


def loop(n, body):
    def step(i, carry):
        body(i)
        return carry

    lax.fori_loop(0, n, step, 0)


def unrolled(n, body):
    for i in range(n):
        body(i)


def kernel(
    img_hbm, wr_hbm, ws_hbm, we_hbm, wp_hbm, wc, mask, label,
    gimg_hbm, o_reduce, o_spatial, o_expand, o_project, o_classify, o_loss,
    wr, ws, we, wp, img, pre, prs, actb, rc_odd, rc_even, evp, evb, colb, col16, hcol, hcor, hcolf, srow,
    psp, spat, ne, npj, r_e, r_p, feat, gb, dnb, eg, pg, dbuf, dcat, wback, eo, natb, prg16,
    dright, dcor, drightf, drow, dcol, ob,
    a_ws, a_we, a_wp, a_wr, a_misc,
    s1, r0, r1, a1, r2, a3, s3, r4, s5, r5, a5, r6, a7, r7,
    sem_in, sem_w, sem_h, sem_g, sem0, sem1, sem2, sem3, sem4, sem5, sem6, sem7, sem8,
):
    row, col, sld = lax.axis_index("row"), lax.axis_index("col"), lax.axis_index("slide")
    grp = row * NS + sld
    has_up, has_down = row > 0, row < NR - 1
    has_left, has_right = col > 0, col < NC - 1

    rows_in = H // IMG_CHUNKS

    def image_copy(k):
        return pltpu.make_async_copy(
            img_hbm.at[0, pl.ds(k * rows_in, rows_in)], img.at[pl.ds(k * rows_in, rows_in)], sem_in.at[k]
        )

    weights = [
        pltpu.make_async_copy(a, b, sem_w.at[k])
        for k, (a, b) in enumerate(((wr_hbm, wr), (ws_hbm, ws), (we_hbm, we), (wp_hbm, wp)))
    ]
    weights[0].start()
    loop(IMG_CHUNKS, lambda k: image_copy(k).start())
    for copy in weights[1:]:
        copy.start()

    def col_peer(d):
        return {"col": lax.rem(col + d, NC)}

    def grp_peer(d):
        q = lax.rem(grp + d, NR * NS)
        return {"row": q // NS, "slide": lax.rem(q, NS)}

    barrier = pltpu.get_barrier_semaphore()
    loop(NC - 1, lambda d: pl.semaphore_signal(barrier, inc=1, device_id=col_peer(d + 1), device_id_type=MESH))
    loop(NR * NS - 1, lambda d: pl.semaphore_signal(barrier, inc=1, device_id=grp_peer(d + 1), device_id_type=MESH))
    to_diag = has_down & has_right
    from_diag = has_up & has_left

    @pl.when(to_diag)
    def _():
        pl.semaphore_signal(barrier, inc=1, device_id={"row": row + 1, "col": col + 1}, device_id_type=MESH)

    @pl.when(from_diag)
    def _():
        pl.semaphore_signal(barrier, inc=1, device_id={"row": row - 1, "col": col - 1}, device_id_type=MESH)

    actb[:, 0:8, :] = jnp.zeros_like(actb[:, 0:8, :])
    dbuf[:, Q : Q + 8, :] = jnp.zeros_like(dbuf[:, Q : Q + 8, :])
    ones_m = jnp.full((CM, CM), 4.0 / CM, BF16)
    ones_o = jnp.full((CM, CM), 4.0 / CO, BF16)

    @pl.when(jnp.logical_not(has_up))
    def _():
        rc_odd[0] = jnp.zeros_like(rc_odd[0])

    @pl.when(jnp.logical_not(has_left))
    def _():
        hcol[...] = jnp.zeros_like(hcol)

    @pl.when(jnp.logical_not(from_diag))
    def _():
        hcor[...] = jnp.zeros_like(hcor)

    @pl.when(jnp.logical_not(has_down))
    def _():
        dcat[Q] = jnp.zeros_like(dcat[Q])

    @pl.when(jnp.logical_not(has_right))
    def _():
        dright[...] = jnp.zeros_like(dright)

    @pl.when(jnp.logical_not(to_diag))
    def _():
        dcor[...] = jnp.zeros_like(dcor)

    drow_w = wc[1:2, :] - wc[0:1, :]
    sign = 1.0 - 2.0 * label[0].astype(F32)
    tissue_all = mask[...].astype(F32)
    tiles = jnp.sum(jnp.sum(tissue_all, axis=0), axis=1, keepdims=True)
    mask_r = lax.broadcasted_iota(jnp.int32, mask.shape, 0)
    mask_c = lax.broadcasted_iota(jnp.int32, mask.shape, 2)

    weights[0].wait()

    def pass1(k):
        image_copy(k).wait()
        x = img[pl.ds(k * 8, 8)].reshape(8 * H, CI)
        v = dot(x, wr[...])
        cut = 192
        by_lane = lax.rsqrt(
            jnp.sum(v[:cut] * v[:cut], axis=-1, keepdims=True) * (4.0 / CM) + 4.0 * EPSILON
        )
        scale = jnp.concatenate(
            [jnp.broadcast_to(by_lane, (cut, CM)), half_scale(v[cut:] * v[cut:], ones_m)], axis=0
        )
        half = v * scale
        pre[pl.ds(k * 8, 8)] = half.reshape(8, H, CM)
        prs[pl.ds(k * 8, 8)] = scale.reshape(8, H, CM)
        actb[:, 8 : 8 + H, :] = silu(half).reshape(8, H, CM)
        for r in range(8):
            rows, at = (rc_even, k * 4 + r // 2) if r % 2 == 0 else (rc_odd, k * 4 + r // 2 + 1)
            for b in range(3):
                rows[at, :, b * CM : (b + 1) * CM] = actb[r, pl.ds(7 + b, Q, stride=2), :].astype(BF16)
            colb[pl.ds(k * 8 + r, 1), :] = actb[r, 7 + H : 8 + H, :]

    loop(IMG_CHUNKS, pass1)

    col16[...] = colb[...].astype(BF16)
    srow[...] = rc_odd[Q]

    def remote(src, dst, send, recv, device):
        return pltpu.make_async_remote_copy(
            src_ref=src, dst_ref=dst, send_sem=send, recv_sem=recv, device_id=device, device_id_type=MESH
        )

    down = remote(srow, rc_odd.at[0], sem_h.at[0], sem_h.at[1], {"row": lax.rem(row + 1, NR)})
    right = remote(col16, hcol, sem_h.at[2], sem_h.at[3], {"col": lax.rem(col + 1, NC)})
    diag = remote(
        col16.at[pl.ds(H - 16, 16)], hcor, sem_h.at[4], sem_h.at[5],
        {"row": lax.rem(row + 1, NR), "col": lax.rem(col + 1, NC)},
    )
    n_diag = jnp.where(to_diag, 1, 0) + jnp.where(from_diag, 1, 0)
    pl.semaphore_wait(barrier, NC - 1 + NR * NS - 1 + n_diag)
    forward = ((down, has_down, has_up), (right, has_right, has_left), (diag, to_diag, from_diag))
    for copy, sends, _ in forward:
        pl.when(sends)(copy.start)

    a_ws[...] = jnp.zeros_like(a_ws)
    a_we[...] = jnp.zeros_like(a_we)
    a_wp[...] = jnp.zeros_like(a_wp)
    a_wr[...] = jnp.zeros_like(a_wr)
    a_misc[...] = jnp.zeros_like(a_misc)
    for copy in weights[1:]:
        copy.wait()
    wback[...] = jnp.zeros_like(wback)

    def tap(a, b):
        return ws[a, b * CM : (b + 1) * CM, :]

    for slot, a in ((0, 1), (1, 2), (2, 0)):
        wback[slot, 0:CM, 0:CM] = tap(a, 1)
        wback[slot, CM : 2 * CM, 0:CM] = tap(a, 2)
        wback[slot, CM : 2 * CM, CM : 2 * CM] = tap(a, 0)
    def even_rows(m):
        x = img[2 * m].astype(F32)
        for half in range(2):
            evb[half] = x[:, half * CM : (half + 1) * CM]
        for half in range(2):
            evp[m, :, half * CM : (half + 1) * CM] = evb[half, pl.ds(0, Q, stride=2), :].astype(BF16)

    loop(Q // 4, lambda m: unrolled(4, lambda i: even_rows(4 * m + i)))

    def project(b):
        at = pl.ds(b * 8 * Q, 8 * Q)
        p = dot(evp[pl.ds(b * 8, 8)].reshape(8 * Q, CI), wp[...])
        npj[at, :] = p
        r_p[at, :] = half_scale(sum(p[:, lanes(k)] * p[:, lanes(k)] for k in range(4)), ones_o)

    loop(2, lambda b: unrolled(3, lambda i: project(3 * b + i)))

    for copy, sends, takes in forward:
        pl.when(takes)(copy.wait_recv)
        pl.when(sends)(copy.wait_send)

    hcolf[0:H] = hcol[...].astype(F32)
    hcolf[H : H + 16] = hcor[...].astype(F32)
    first = lax.broadcasted_iota(jnp.int32, (16, CM), 0) == 0

    def patch_left(rows, at, value):
        old = rows[at, 0:16, 0:CM].astype(F32)
        rows[at, 0:16, 0:CM] = jnp.where(first, value, old).astype(BF16)

    patch_left(rc_odd, 0, hcolf[H + 15 : H + 16, :])

    def patch_rows(m):
        patch_left(rc_even, m, hcolf[pl.ds(2 * m, 1), :])
        patch_left(rc_odd, m + 1, hcolf[pl.ds(2 * m + 1, 1), :])

    loop(Q // 4, lambda m: unrolled(4, lambda i: patch_rows(4 * m + i)))

    ng = NR * NS

    def start(n, make):
        loop(n, lambda d: make(d + 1).start())

    def finish(n, make):
        loop(n, lambda d: make(d + 1).wait())

    def chunk(p):
        return pl.ds(pl.multiple_of(p * CHUNK, CHUNK), CHUNK)

    def piece(p):
        return pl.ds(pl.multiple_of(p * PIECE, PIECE), PIECE)

    core, cy = lax.rem(col, 2), col // 2
    half_rows = NC // 2 * CHUNK

    def y_chunk(y):
        return chunk(core * (NC // 2) + y)

    other = {"col": col + 1 - 2 * core}

    def scatter0(part):
        size = half_rows // 2
        src = s1.at[pl.ds(pl.multiple_of((1 - core) * half_rows + part * size, size), size)]
        return remote(src, r0.at[pl.ds(part * size, size)], sem0.at[0, part], sem0.at[1, part], other)

    def add_part(part):
        scatter0(part).wait()
        for y in (2 * part, 2 * part + 1):
            mine = y_chunk(y)
            s1[mine, :] = (s1[mine, :].astype(F32) + r0[y * CHUNK : (y + 1) * CHUNK, :].astype(F32)).astype(BF16)
        for d in range(1, NC // 2):
            pl.when(lax.rem(cy + d, NC // 2) // 2 == part)(scatter1(d).start)

    def scatter1(d):
        peer = lax.rem(cy + d, NC // 2)
        return remote(s1.at[y_chunk(peer)], r1.at[cy], sem1.at[0, d], sem1.at[1, d], {"col": 2 * peer + core})

    def scatter2(d):
        q = lax.rem(grp + d, ng)
        return remote(a1.at[piece(q)], r2.at[grp], sem2.at[0, d], sem2.at[1, d], grp_peer(d))

    def gather3(d):
        return remote(a3.at[piece(grp)], a3.at[piece(grp)], sem3.at[0, d], sem3.at[1, d], grp_peer(d))

    def gather4(d):
        peer = lax.rem(cy + d, NC // 2)
        return remote(s3, r4.at[y_chunk(cy)], sem4.at[0, d], sem4.at[1, d], {"col": 2 * peer + core})

    def gather8(d):
        there = r4.at[y_chunk(lax.rem(cy - d + NC // 2, NC // 2))]
        return remote(there, there, sem8.at[0, d], sem8.at[1, d], other)

    def scatter5(d):
        peer = lax.rem(col + d, NC)
        return remote(s5.at[peer], r5.at[col], sem5.at[0, d], sem5.at[1, d], {"col": peer})

    def gather6(d):
        return remote(a5, r6.at[grp], sem6.at[0, d], sem6.at[1, d], grp_peer(d))

    def gather7(d):
        return remote(a7, r7.at[col], sem7.at[0, d], sem7.at[1, d], col_peer(d))

    npx = TB * Q

    def taps(a, at, n):
        if a == 1:
            return rc_even[pl.ds(at, n)].reshape(n * Q, 3 * CM)
        return rc_odd[pl.ds(at + a // 2, n)].reshape(n * Q, 3 * CM)

    def spatial_weight_grad(u):
        d16 = dcat[pl.ds(u * TB, TB), :, 0:CM].reshape(npx, CM)
        for a in range(3):
            a_ws[:, a * 3 * CM : (a + 1) * 3 * CM] += dot_tn(d16, taps(a, u * TB, TB))

    def tile_row(u):
        i0 = u * TB

        def convolve(b):
            at = i0 + b * 8
            v = sum(dot(taps(a, at, 8), ws[a]) for a in range(3))
            scale = half_scale(v * v, ones_m)
            half = v * scale
            psp[0, pl.ds(b * 8 * Q, 8 * Q), :] = half
            psp[1, pl.ds(b * 8 * Q, 8 * Q), :] = scale
            spat[pl.ds(b * 8 * Q, 8 * Q), :] = silu(half).astype(BF16)

        unrolled(2, convolve)

        def expand(b):
            at = pl.ds(b * 8 * Q, 8 * Q)
            e = dot(spat[at, :], we[...])
            ne[at, :] = e
            r_e[at, :] = half_scale(sum(e[:, lanes(k)] * e[:, lanes(k)] for k in range(4)), ones_o)

        unrolled(2, expand)
        feat[...] = jnp.zeros_like(feat)

        def merge(b):
            at = pl.ds(b * 4 * Q, 4 * Q)
            out = pl.ds(i0 * Q + b * 4 * Q, 4 * Q)
            h_e, h_p = r_e[at, :], r_p[out, :]
            for k in range(4):
                half = ne[at, lanes(k)] * h_e + npj[out, lanes(k)] * h_p
                feat[:, lanes(k)] += jnp.sum(silu(half).reshape(4, Q, CM), axis=0)

        loop(4, merge)

        for v in range(3):
            f = jnp.sum(feat[v * TB : (v + 1) * TB, :], axis=0, keepdims=True) * (1.0 / (TB * TB))
            margin = jnp.sum(f * drow_w, axis=1, keepdims=True) * sign
            here = (mask_r == row * 3 + u) & (mask_c == col * 3 + v)
            tissue = jnp.where(here, tissue_all, 0.0)
            tissue = jnp.sum(jnp.sum(tissue, axis=0), axis=1, keepdims=True)
            soft = jnp.maximum(margin, 0.0) + jnp.log(1.0 + jnp.exp(-jnp.abs(margin)))
            weight = tissue * (0.5 + 0.5 * jnp.tanh(0.5 * margin)) / tiles * sign
            for k in range(CO // CM):
                a_misc[k : k + 1, :] += f[:, k * CM : (k + 1) * CM] * weight
            a_misc[4:5, :] += jnp.broadcast_to(tissue * soft / tiles, (1, CM))
            gb[v * TB : (v + 1) * TB, :] = jnp.broadcast_to(drow_w * (weight * 288.0), (TB, CO))

        def unmerge(b):
            at = pl.ds(b * 4 * Q, 4 * Q)
            out = pl.ds(i0 * Q + b * 4 * Q, 4 * Q)
            s_e, s_p = r_e[at, :], r_p[out, :]
            z_e, z_p = 0.0, 0.0
            for k in range(4):
                n_e, n_p = ne[at, lanes(k)] * s_e, npj[out, lanes(k)] * s_p
                dn = silu_vjp((n_e + n_p).reshape(4, Q, CM), gb[:, lanes(k)][None]).reshape(4 * Q, CM)
                dnb[:, lanes(k)] = dn
                z_e, z_p = z_e + dn * n_e, z_p + dn * n_p
            m_e, m_p = lane_mean(z_e, ones_o), lane_mean(z_p, ones_o)
            for k in range(4):
                dn = dnb[:, lanes(k)]
                n_e, n_p = ne[at, lanes(k)] * s_e, npj[out, lanes(k)] * s_p
                eg[at, lanes(k)] = (s_e * (dn - n_e * m_e)).astype(BF16)
                pg[out, lanes(k)] = (s_p * (dn - n_p * m_p)).astype(BF16)

        loop(4, unmerge)

        a_we[...] += dot_tn(spat[...], eg[...])
        a_wp[...] += dot_tn(evp[pl.ds(i0, TB)].reshape(npx, CI), pg[pl.ds(i0 * Q, npx), :])

    def back_row(u):
        i0 = u * TB

        def unconvolve(b):
            at = pl.ds(b * 8 * Q, 8 * Q)
            g = dot_nt(eg[at, :], we[...])
            d = act_vjp(psp[0, at, :], psp[1, at, :], g, ones_m)
            dbuf[:, 0:Q, :] = d.reshape(8, Q, CM)
            d16 = d.astype(BF16)
            dcat[pl.ds(i0 + b * 8, 8), :, 0:CM] = d16.reshape(8, Q, CM)
            for r in range(8):
                dcat[i0 + b * 8 + r, :, CM : 2 * CM] = dbuf[r, 1 : Q + 1, :].astype(BF16)
                dcol[pl.ds(i0 + b * 8 + r, 1), :] = dbuf[r, 0:1, :]

        unrolled(2, unconvolve)

    def both(u):
        tile_row(u)
        back_row(u)
        spatial_weight_grad(u)

    e_slot, s_slot = (0, 1, 4, 5), (2, 3, 6)

    def e_rows(r):
        at = e_slot[r // CHUNK] * CHUNK + r % CHUNK
        return slice(at, at + CM)

    def s_rows(t):
        at = s_slot[t // 3] * CHUNK + t % 3 * CM
        return slice(at, at + CM)

    loop(2, both)
    tile_row(2)
    for q in range(4):
        s1[e_rows(q * CM), :] = a_we[:, lanes(q)].astype(BF16)
        for part in range(2):
            s1[e_rows(512 + (2 * q + part) * CM), :] = a_wp[part * CM : (part + 1) * CM, lanes(q)].astype(BF16)
    s1[7 * CHUNK :, :] = jnp.zeros((CHUNK, CM), BF16)
    scatter0(0).start()
    back_row(2)

    drow[...] = dcat[0]
    col16[0:Q] = dcol[...].astype(BF16)
    up = remote(drow, dcat.at[Q], sem_g.at[0], sem_g.at[1], {"row": lax.rem(row + NR - 1, NR)})
    left = remote(col16.at[pl.ds(0, Q)], dright, sem_g.at[2], sem_g.at[3], {"col": lax.rem(col + NC - 1, NC)})
    gaid = remote(
        col16.at[pl.ds(0, 16)], dcor, sem_g.at[4], sem_g.at[5],
        {"row": lax.rem(row + NR - 1, NR), "col": lax.rem(col + NC - 1, NC)},
    )
    backward = ((up, has_up, has_down), (left, has_left, has_right), (gaid, from_diag, to_diag))
    for copy, sends, _ in backward:
        pl.when(sends)(copy.start)

    add_part(0)
    spatial_weight_grad(2)
    for t in range(9):
        s1[s_rows(t), :] = a_ws[:, lanes(t)].T.astype(BF16)
    scatter0(1).start()
    add_part(1)
    for copy, sends, takes in backward:
        pl.when(takes)(copy.wait_recv)
        pl.when(sends)(copy.wait_send)

    drightf[0:Q] = dright[...].astype(F32)
    drightf[Q : Q + 16] = dcor[...].astype(F32)
    last = lax.broadcasted_iota(jnp.int32, (16, CM), 0) == 15

    def patch_right(at, value):
        old = dcat[at, Q - 16 : Q, CM : 2 * CM].astype(F32)
        dcat[at, Q - 16 : Q, CM : 2 * CM] = jnp.where(last, value, old).astype(BF16)

    loop(Q, lambda m: patch_right(m, drightf[pl.ds(m, 1), :]))
    patch_right(Q, drightf[Q : Q + 1, :])

    def pass3(b):
        i0 = b * 8
        here = dcat[pl.ds(i0, 8)].reshape(8 * Q, 2 * CM)
        below = dcat[pl.ds(i0 + 1, 8)].reshape(8 * Q, 2 * CM)
        eo[0] = dot_nt(here, wback[0]).reshape(8, Q, 2 * CM)
        eo[1] = (dot_nt(here, wback[1]) + dot_nt(below, wback[2])).reshape(8, Q, 2 * CM)

        def some_rows(c):
            for rp in range(2):
                at = 2 * (i0 + 4 * c)
                for cp in range(2):
                    half, scale = (
                        jnp.concatenate([ref[at + 2 * i + rp, pl.ds(cp, Q, stride=2), :] for i in range(4)], axis=0)
                        for ref in (pre, prs)
                    )
                    g = eo[rp, pl.ds(4 * c, 4), :, lanes(cp)].reshape(4 * Q, CM)
                    d = act_vjp(half, scale, g, ones_m)
                    for i in range(4):
                        natb[rp, i, pl.ds(cp, Q, stride=2), :] = d[i * Q : (i + 1) * Q]
                for i in range(4):
                    prg16[at + 2 * i + rp] = natb[rp, i].astype(BF16)

        unrolled(2, some_rows)
        rows = pl.ds(2 * i0, 16)
        a_wr[...] += dot_tn(prg16[rows].reshape(16 * H, CM), img[rows].reshape(16 * H, CI))

    loop(3, pass3)
    finish(NC // 2 - 1, scatter1)
    r1[cy] = s1[y_chunk(cy), :]
    a1[...] = sum(r1[p].astype(F32) for p in range(NC // 2))
    start(ng - 1, scatter2)
    loop(3, lambda b: pass3(b + 3))

    for p in range(NC):
        s5[p, 32:40, :] = jnp.zeros((8, CM), F32)
        if p < 5:
            s5[p, 32:33, :] = a_misc[p : p + 1, :]
    for half in range(2):
        t = a_wr[:, lanes(half)].T * SCALE
        for p in range(4):
            s5[half * 4 + p, 0:32, :] = t[p * 32 : (p + 1) * 32, :]

    def pass4(k):
        main = dot_nt(prg16[pl.ds(k * 8, 8)].reshape(8 * H, CM), wr[...])
        side = dot_nt(pg[pl.ds(k * 4 * Q, 4 * Q), :], wp[...])
        for m in range(4):
            at = k * 8 + 2 * m
            for half in range(2):
                ob[half, m] = main[2 * m * H : (2 * m + 1) * H, lanes(half)]
                ob[half, m, pl.ds(0, Q, stride=2), :] += side[m * Q : (m + 1) * Q, lanes(half)]
                gimg_hbm[0, at, :, lanes(half)] = ob[half, m].astype(BF16)
            gimg_hbm[0, at + 1] = main[(2 * m + 1) * H : (2 * m + 2) * H].astype(BF16)

    def some(lo, hi):
        loop(hi - lo, lambda k: pass4(lo + k))

    finish(ng - 1, scatter2)
    r2[grp] = a1[piece(grp), :]
    a3[piece(grp), :] = sum(r2[p] for p in range(ng)) * SCALE
    start(ng - 1, gather3)
    start(NC - 1, scatter5)
    some(0, 4)
    finish(NC - 1, scatter5)
    r5[col] = s5[col]
    a5[...] = sum(r5[p] for p in range(NC))
    r6[grp] = a5[...]
    start(ng - 1, gather6)
    some(4, 6)
    finish(ng - 1, gather3)
    s3[...] = a3[...].astype(BF16)
    r4[y_chunk(cy), :] = s3[...]
    start(NC // 2 - 1, gather4)
    gather8(0).start()
    some(6, 9)
    finish(ng - 1, gather6)
    a7[...] = sum(r6[p] for p in range(ng))
    r7[col] = a7[...]
    start(NC - 1, gather7)
    some(9, 12)
    for d in range(1, NC // 2):
        gather4(d).wait_recv()
        gather8(d).start()
    finish(NC - 1, gather7)
    for d in range(1, NC // 2):
        gather4(d).wait_send()
    for d in range(NC // 2):
        gather8(d).wait()

    for t in range(9):
        o_spatial[t * CM : (t + 1) * CM, :] = r4[s_rows(t), :].astype(F32)
    for q in range(4):
        o_expand[:, lanes(q)] = r4[e_rows(q * CM), :].astype(F32)
        for part in range(2):
            o_project[part * CM : (part + 1) * CM, lanes(q)] = r4[e_rows(512 + (2 * q + part) * CM), :].astype(F32)
    for p in range(NC):
        o_reduce[p * 32 : (p + 1) * 32, :] = r7[p, 0:32, :]
    for k in range(4):
        o_classify[0:1, lanes(k)] = -r7[k, 32:33, :]
        o_classify[1:2, lanes(k)] = r7[k, 32:33, :]
    o_loss[...] = r7[4, 32:33, 0:1]


def hand_over(*refs):
    n = (len(refs) - 1) // 2
    given, taken, sem = refs[:n], refs[n : 2 * n], refs[-1]
    copies = [pltpu.make_async_copy(a, b, sem.at[k]) for k, (a, b) in enumerate(zip(given, taken))]
    for c in copies:
        c.start()
    for c in copies:
        c.wait()


def per_device(image, wr, ws, we, wp, wc, mask, label):
    vmem = pl.BlockSpec(memory_space=pltpu.VMEM)
    hbm = pl.BlockSpec(memory_space=pl.ANY)
    v = pltpu.VMEM
    dma = pltpu.SemaphoreType.DMA
    scratch = [
        v((CI, CM), BF16),
        v((3, 3 * CM, CM), BF16),
        v((CM, CO), BF16),
        v((CI, CO), BF16),
        v((H, H, CI), BF16),
        v((H, H, CM), F32),
        v((H, H, CM), F32),
        v((8, 8 + H, CM), F32),
        v((Q + 1, Q, 3 * CM), BF16),
        v((Q, Q, 3 * CM), BF16),
        v((Q, Q, CI), BF16),
        v((2, H, CM), F32),
        v((H, CM), F32),
        v((H, CM), BF16),
        v((H, CM), BF16),
        v((16, CM), BF16),
        v((H + 16, CM), F32),
        v((Q, 3 * CM), BF16),
        v((2, TB * Q, CM), F32),
        v((TB * Q, CM), BF16),
        v((TB * Q, CO), F32),
        v((Q * Q, CO), F32),
        v((TB * Q, CM), F32),
        v((Q * Q, CM), F32),
        v((Q, CO), F32),
        v((Q, CO), F32),
        v((4 * Q, CO), F32),
        v((TB * Q, CO), BF16),
        v((Q * Q, CO), BF16),
        v((8, Q + 8, CM), F32),
        v((Q + 1, Q, 2 * CM), BF16),
        v((3, 2 * CM, 2 * CM), BF16),
        v((2, 8, Q, 2 * CM), F32),
        v((2, 4, H, CM), F32),
        v((H, H, CM), BF16),
        v((Q, CM), BF16),
        v((16, CM), BF16),
        v((Q + 16, CM), F32),
        v((Q, 2 * CM), BF16),
        v((Q, CM), F32),
        v((2, 4, H, CM), F32),
        v((CM, 9 * CM), F32),
        v((CM, CO), F32),
        v((CI, CO), F32),
        v((CM, CI), F32),
        v((8, CM), F32),
        v((NC * CHUNK, CM), BF16),
        v((NC // 2 * CHUNK, CM), BF16),
        v((NC // 2, CHUNK, CM), BF16),
        v((CHUNK, CM), F32),
        v((NR * NS, PIECE, CM), F32),
        v((CHUNK, CM), F32),
        v((CHUNK, CM), BF16),
        v((NC * CHUNK, CM), BF16),
        v((NC, 40, CM), F32),
        v((NC, 40, CM), F32),
        v((40, CM), F32),
        v((NR * NS, 40, CM), F32),
        v((40, CM), F32),
        v((NC, 40, CM), F32),
        dma((IMG_CHUNKS,)),
        dma((4,)),
        dma((6,)),
        dma((6,)),
        dma((2, 2)),
        dma((2, NC)),
        dma((2, NR * NS)),
        dma((2, NR * NS)),
        dma((2, NC)),
        dma((2, NC)),
        dma((2, NR * NS)),
        dma((2, NC)),
        dma((2, NC)),
    ]
    shapes = [image.shape, (CI, CM), (9 * CM, CM), (CM, CO), (CI, CO), (2, CO), (1, 1)]
    out = pl.pallas_call(
        kernel,
        out_shape=[v(s, BF16 if k == 0 else F32) for k, s in enumerate(shapes)],
        in_specs=[hbm] * 5 + [vmem] * 2 + [pl.BlockSpec(memory_space=pltpu.SMEM)],
        out_specs=[vmem] * 7,
        scratch_shapes=scratch,
        compiler_params=pltpu.CompilerParams(
            collective_id=0, has_side_effects=True, vmem_limit_bytes=50 * 1024 * 1024
        ),
        cost_estimate=pl.CostEstimate(flops=7_000_000_000, bytes_accessed=12_000_000, transcendentals=4_000_000),
    )(image, wr, ws.reshape(3, 3 * CM, CM), we, wp, wc.T, jnp.transpose(mask, (1, 0, 2)), label)
    out = pl.pallas_call(
        hand_over,
        out_shape=[jax.ShapeDtypeStruct(o.shape, o.dtype) for o in out],
        in_specs=[vmem] * len(out),
        out_specs=[hbm] * len(out),
        scratch_shapes=[dma((len(out),))],
        compiler_params=pltpu.CompilerParams(vmem_limit_bytes=1024 * 1024),
    )(*out)
    grad_image, g_reduce, g_spatial, g_expand, g_project, g_classify, loss = out
    return grad_image, g_reduce, g_spatial.reshape(3, 3, CM, CM), g_expand, g_project, g_classify.T, loss[0, 0]


def solution(mesh):
    in_specs = (P("slide", "row", "col", None), P(), P(), P(), P(), P(), P("slide", None, None), P("slide"))
    out_specs = (P("slide", "row", "col", None), P(), P(), P(), P(), P(), P())
    return jax.shard_map(per_device, mesh=mesh, in_specs=in_specs, out_specs=out_specs, check_vma=False)
```
